512 devices in a mesh: fsdp: 128 (over z, y, core), rep: 4 (over x).
Axes of the slice: x: 4, y: 8, z: 8, core: 2. Of those that a mesh axis runs over, the one named last changes fastest.
Arguments:
- replica_grads: bfloat16 [4, 512, 65536], P('rep', 'fsdp'), may hold values from -18 to 18
- momentum: float32 [512, 65536], P('fsdp', 'rep'), may hold values from -6 to 6
- second_moment: float32 [512, 65536], P('fsdp', 'rep'), may hold values from 0.0001 to 1
- factor_stats: float32 [128, 4, 512, 512], P('fsdp', 'rep'), may hold values from -0.1 to 16.2, as said below
- block_owner: int32 [128], replicated, may hold values from 0 to 127, as said below
- block_offset: int32 [128], replicated, may hold values from 0 to 127, each once
Outputs:
- new_momentum: float32 [512, 65536], P('fsdp', 'rep')
- new_second: float32 [512, 65536], P('fsdp', 'rep')
- new_factors: float32 [128, 4, 512, 512], P('fsdp', 'rep')
The draws below stay inside these ranges and needn't reach their ends.
Inputs may be any that keep to these rules, and one draw needn't show every extreme that they name: `block_owner`: each fsdp index owns at most 2 blocks; exactly 32 indices own two blocks, 64 own one, the others none. `factor_stats`: symmetric.
All inputs are finite; a program needn't handle non-finite values.
Results may differ from the reference program's by a relative error of at most 0.017.
Values may be sent and summed in bfloat16 or wider, within the bound.
A program may use at most 128 MiB of HBM per device.

```python
import math
import jax
import jax.numpy as jnp
from jax import lax

BS = 512
ITERS = 3
NBLK = 128
WIDTH = 65536
N_FSDP = 128
N_REP = 4


def draw_replica_grads(key, part):
    key = jax.random.fold_in(key, 11)
    key_rows, key_cols, key_common = jax.random.split(key, 3)
    ramp = jnp.arange(BS, dtype=jnp.float32) / BS
    jitter = jax.random.uniform(key_rows, (BS,), jnp.float32, math.log(0.5), math.log(2.0))
    row_scale = jnp.exp(ramp * math.log(10.0) + jitter)
    col_scale = jnp.exp(jax.random.uniform(key_cols, (WIDTH,), jnp.float32, 0.0, math.log(10.0)))
    base = jnp.clip(jax.random.normal(key_common, (N_REP, BS, WIDTH), jnp.float32), -6.0, 6.0)
    magnitude = 0.01
    values = magnitude * row_scale[None, :, None] * col_scale[None, None, :] * base
    return values.astype(jnp.bfloat16)


def draw_factor_stats(key, part):
    key = jax.random.fold_in(key, 23)
    key_diag, key_off = jax.random.split(key, 2)
    diagonal = jnp.exp(jax.random.uniform(key_diag, (N_FSDP, N_REP, BS), jnp.float32, math.log(2.0), math.log(8.0)))
    noise = jax.random.uniform(key_off, (N_FSDP, N_REP, BS, BS), jnp.float32, -0.1, 0.1)
    symmetric = 0.5 * (noise + jnp.swapaxes(noise, -1, -2))
    identity = jnp.eye(BS, dtype=jnp.float32)
    return symmetric + diagonal[..., None] * identity


def draw_block_owner(key, part):
    key = jax.random.fold_in(key, 5)
    key_inner, key_used, key_shuffle = jax.random.split(key, 3)
    quarter = NBLK // 4
    inner = (1 + jax.random.permutation(key_inner, N_FSDP - 2)).astype(jnp.int32)
    ends = jnp.array([0, N_FSDP - 1], dtype=jnp.int32)
    used = jnp.concatenate([inner[quarter:], ends])
    used = used[jax.random.permutation(key_used, used.shape[0])]
    doubles = used[:quarter]
    singles = used[quarter:quarter + NBLK // 2]
    listing = jnp.concatenate([doubles, doubles, singles])
    shuffle = jax.random.permutation(key_shuffle, NBLK)
    return listing[shuffle].astype(jnp.int32)


def levels(stream_key, shape, cuts, low, top_value):
    def one(dim, shards_of):
        steps = jax.random.uniform(jax.random.fold_in(jax.random.fold_in(stream_key, 6), dim), (shards_of,), jnp.float32, low / len(cuts), top_value / len(cuts))
        return jnp.repeat(jnp.exp(steps), shape[dim] // shards_of).reshape((-1,) + (1,) * (len(shape) - dim - 1))

    gain = one(*cuts[0])
    for cut in cuts[1:]:
        gain = gain * one(*cut)
    return gain


def scatter_about(stream_key, extent, spread, bound, pieces=(), kind=jnp.bfloat16):
    level = levels(stream_key, extent, pieces, -0.22, 0.18) if pieces else 1.0
    values = jax.random.normal(stream_key, extent, jnp.float32) * spread * level
    return jnp.minimum(jnp.maximum(values, -bound), bound).astype(kind)


def setup_inputs(seed: int = 0) -> dict:
    key_of = jax.random.split(jax.random.key(seed), 7)
    return {
        "replica_grads": draw_replica_grads(jax.random.fold_in(key_of[6], 71), 0),
        "momentum": scatter_about(key_of[1], (BS, WIDTH), 1.0, 6.0, ((0, 128), (1, 4)), jnp.float32),
        "second_moment": jnp.clip(jnp.exp(math.log(1.0) - 9.2103404 * jax.random.uniform(key_of[2], (BS, WIDTH), jnp.float32) ** levels(key_of[2], (BS, WIDTH), ((0, 128), (1, 4)), -0.2, 0.2)), 0.0001, 1.0),
        "factor_stats": draw_factor_stats(jax.random.fold_in(key_of[6], 71), 0),
        "block_owner": draw_block_owner(jax.random.fold_in(key_of[6], 71), 0),
        "block_offset": jax.random.permutation(key_of[5], NBLK).astype(jnp.int32),
    }


FACTOR_DECAY = 0.95
MATRIX_EPS = 1e-06
ADAM_DECAY = 0.99
ADAM_EPS = 1e-08
NORM_EPS = 1e-06
MOMENTUM_DECAY = 0.9

def matmul_high(left, right):
    return jnp.dot(left, right, precision=lax.Precision.HIGHEST, preferred_element_type=jnp.float32)

def inverse_root(matrix):
    identity = jnp.eye(matrix.shape[0], dtype=jnp.float32)
    frobenius = jnp.sqrt(jnp.sum(matrix * matrix))
    scaling = 2.5 / frobenius
    coupled = scaling * matrix
    iterate = identity
    for section in range(ITERS):
        poly_step = (5.0 * identity - coupled) * 0.25
        if section == 0:
            iterate = jnp.sqrt(jnp.sqrt(scaling)) * poly_step
        else:
            iterate = matmul_high(iterate, poly_step)
        if section + 1 < ITERS:
            squared = matmul_high(poly_step, poly_step)
            coupled = matmul_high(matmul_high(squared, squared), coupled)
    return iterate

def slot_ranks(block_owner):
    positions = jnp.arange(block_owner.shape[0], dtype=jnp.int32)
    same_owner = block_owner[:, None] == block_owner[None, :]
    earlier = positions[None, :] < positions[:, None]
    return lax.optimization_barrier(jnp.sum((same_owner & earlier).astype(jnp.int32), axis=1)).astype(jnp.int32)

def reference(replica_grads, momentum, second_moment, factor_stats, block_owner, block_offset):
    gradient = lax.optimization_barrier(jnp.sum(replica_grads.astype(jnp.float32), axis=0)).astype(jnp.bfloat16)
    grad_wide = gradient.astype(jnp.float32)
    new_second = ADAM_DECAY * second_moment + (1.0 - ADAM_DECAY) * grad_wide * grad_wide
    adam_dir = grad_wide / (jnp.sqrt(new_second) + ADAM_EPS)
    ranking = slot_ranks(block_owner)
    identity = jnp.eye(BS, dtype=jnp.float32)

    def one_block(state_carry, scan_item):
        stats, update = state_carry
        owner, ranked, offset = scan_item
        column = (offset * BS).astype(jnp.int32)
        block_grad = lax.dynamic_slice_in_dim(gradient, column, BS, 1)
        adam_block = lax.dynamic_slice_in_dim(adam_dir, column, BS, 1)
        graft_sq = jnp.sum(adam_block * adam_block)
        left_stat = jnp.dot(block_grad, block_grad.T, preferred_element_type=jnp.float32)
        right_stat = jnp.dot(block_grad.T, block_grad, preferred_element_type=jnp.float32)
        left_new = FACTOR_DECAY * factor_stats[owner, 2 * ranked] + (1.0 - FACTOR_DECAY) * left_stat
        right_new = FACTOR_DECAY * factor_stats[owner, 2 * ranked + 1] + (1.0 - FACTOR_DECAY) * right_stat
        stats = stats.at[owner, 2 * ranked].set(left_new)
        stats = stats.at[owner, 2 * ranked + 1].set(right_new)
        left_root = inverse_root(left_new + MATRIX_EPS * identity).astype(jnp.bfloat16)
        right_root = inverse_root(right_new + MATRIX_EPS * identity).astype(jnp.bfloat16)
        halfway = jnp.dot(left_root, block_grad, preferred_element_type=jnp.float32).astype(jnp.bfloat16)
        precond = jnp.dot(halfway, right_root, preferred_element_type=jnp.float32)
        prec_sq = jnp.sum(precond * precond)
        grafted = (precond * jnp.sqrt(graft_sq / (prec_sq + NORM_EPS))).astype(jnp.bfloat16)
        update = lax.dynamic_update_slice_in_dim(update, grafted, column, 1)
        return ((stats, update), None)
    start = (FACTOR_DECAY * factor_stats, jnp.zeros((BS, WIDTH), jnp.bfloat16))
    finished, _unused = lax.scan(one_block, start, (block_owner, ranking, block_offset))
    new_factors, update = finished
    new_momentum = MOMENTUM_DECAY * momentum + update.astype(jnp.float32)
    return (new_momentum, new_second, new_factors)
```

```python
import jax
import jax.numpy as jnp
from jax import lax
from jax.experimental import pallas as pl
from jax.experimental.pallas import tpu as pltpu
from jax.sharding import PartitionSpec as P

FACTOR_DECAY = 0.95
MATRIX_EPS = 1e-06
ADAM_DECAY = 0.99
ADAM_EPS = 1e-08
NORM_EPS = 1e-06
MOMENTUM_DECAY = 0.9

NF = 128
NR = 4
BS = 512
NBLK = 128
QB = NBLK // NR
HALF = NF // 2
MESH = pl.DeviceIdType.MESH
F32 = jnp.float32
BF16 = jnp.bfloat16


def dot32(left, right):
    return jnp.dot(left, right, preferred_element_type=F32)


def outer_left(mat):
    return lax.dot_general(mat, mat, (((1,), (1,)), ((), ())), preferred_element_type=F32)


def outer_right(mat):
    return lax.dot_general(mat, mat, (((0,), (0,)), ((), ())), preferred_element_type=F32)


def eye_mask():
    return lax.broadcasted_iota(jnp.int32, (BS, BS), 0) == lax.broadcasted_iota(
        jnp.int32, (BS, BS), 1
    )


def plus_diag(mat, value):
    return mat + jnp.where(eye_mask(), value, 0.0)


def roots_of(mats):
    norms = [jnp.sum(jnp.sum(m * m, axis=0, keepdims=True), axis=1, keepdims=True) for m in mats]
    scales = [2.5 / jnp.sqrt(n) for n in norms]
    coupled0 = [z * m for z, m in zip(scales, mats)]

    def next_coupled(coupled, rounded):
        square = [dot32(m, m) for m in rounded]
        inner = [s * 0.0625 - 0.625 * m for s, m in zip(square, coupled)]
        inner_b = [e.astype(BF16) for e in inner]
        fourth = [dot32(e, e) for e in inner_b]
        rest = [(q + 3.125 * e).astype(BF16) for q, e in zip(fourth, inner)]
        return [
            dot32(w, m) + (625.0 / 256.0) * c for w, m, c in zip(rest, rounded, coupled)
        ]

    rounded0 = [m.astype(BF16) for m in coupled0]
    coupled1 = next_coupled(coupled0, rounded0)
    rounded1 = [m.astype(BF16) for m in coupled1]
    pair = [
        (dot32(a, b) - 5.0 * (c + d)) * 0.0625
        for a, b, c, d in zip(rounded0, rounded1, coupled0, coupled1)
    ]
    coupled2 = next_coupled(coupled1, rounded1)
    out = []
    for u, m, z in zip(pair, coupled2, scales):
        last = 5.0 * u - (25.0 / 16.0) * m - dot32(u.astype(BF16), m.astype(BF16))
        root = plus_diag(last * 0.25, 125.0 / 64.0) * jnp.sqrt(jnp.sqrt(z))
        out.append(root.astype(BF16))
    return out


def kernel(
    tab,
    grads,
    mom_in,
    sec_in,
    fac_in,
    newmom_out,
    newsec_out,
    newfac_out,
    mom,
    sec,
    fac,
    newmom,
    newsec,
    newfac,
    gq,
    rs,
    full,
    out,
    arrived,
    block,
    block_x,
    fac_b,
    fac_x,
    ret,
    retbuf,
    xs,
    xr,
    prow,
    zbuf,
    yrow,
    ybuf,
    crow,
    cbuf,
    lsem,
    osem,
    rs_s,
    rs_r,
    ag_s,
    ag_r,
    fx_s,
    fx_r,
    gx_s,
    gx_r,
    a_s,
    a_r,
    b_s,
    b_r,
    x_s,
    x_r,
    z_s,
    z_r,
    y_s,
    y_r,
    c_s,
    c_r,
):
    f = lax.axis_index("fsdp")
    r = lax.axis_index("rep")
    par = lax.rem(r, 2)
    slot = lax.div(r, 2)
    partner = r + 1 - 2 * par
    f_par = lax.rem(f, 2)
    my_j = lax.div(f, 2)
    primary = f_par == par
    other = f_par != par

    def remote(src, dst, send, recv, device):
        return pltpu.make_async_remote_copy(
            src_ref=src,
            dst_ref=dst,
            send_sem=send,
            recv_sem=recv,
            device_id=device,
            device_id_type=MESH,
        )

    def ahead(d):
        return lax.rem(r + d, NR)

    def behind(d):
        return lax.rem(r + NR - d, NR)

    load_g = pltpu.make_async_copy(grads.at[pl.ds(r * QB, QB)], gq, lsem.at[0])
    load_sec = pltpu.make_async_copy(sec_in, sec, lsem.at[1])
    load_fac = pltpu.make_async_copy(fac_in, fac, lsem.at[2])
    load_mom = pltpu.make_async_copy(mom_in, mom, lsem.at[3])
    load_g.start()
    load_sec.start()
    load_fac.start()
    load_mom.start()

    barrier = pltpu.get_barrier_semaphore()
    for d in range(1, NR):
        pl.semaphore_signal(barrier, inc=1, device_id=(f, ahead(d)), device_id_type=MESH)

    def greet(t, carry):
        pl.semaphore_signal(
            barrier, inc=1, device_id=(lax.rem(f + t, NF), r), device_id_type=MESH
        )
        return carry

    lax.fori_loop(1, NF, greet, 0)
    pl.semaphore_wait(barrier, NF - 1 + NR - 1)

    rs_copies = []
    for d in range(1, NR):
        copy = remote(
            grads.at[pl.ds(ahead(d) * QB, QB)],
            rs.at[d - 1],
            rs_s.at[d - 1],
            rs_r.at[d - 1],
            (f, ahead(d)),
        )
        copy.start()
        rs_copies.append(copy)
    load_fac.wait()

    @pl.when(other)
    def _():
        fac_b[...] = fac[...].astype(BF16)

    load_g.wait()
    for copy in rs_copies:
        copy.wait_recv()
    total = gq[...].astype(F32)
    for d in range(1, NR):
        total = total + rs[d - 1].astype(F32)
    mine = total.astype(BF16)
    full[pl.ds(r * QB, QB)] = mine

    for d in range(1, NR):
        remote(
            full.at[pl.ds(r * QB, QB)],
            full.at[pl.ds(r * QB, QB)],
            ag_s.at[d - 1],
            ag_r.at[d - 1],
            (f, ahead(d)),
        ).start()

    @pl.when(other)
    def _():
        remote(fac_b, fac_x, fx_s, fx_r, (f, partner)).start()

    load_sec.wait()
    wide = mine.astype(F32)
    second = ADAM_DECAY * sec[...] + (1.0 - ADAM_DECAY) * wide * wide
    newsec[...] = second
    store_sec = pltpu.make_async_copy(newsec, newsec_out, osem.at[0])
    store_sec.start()
    direction = wide / (jnp.sqrt(second) + ADAM_EPS)
    lanes = jnp.sum(direction * direction, axis=1)
    sums = jnp.sum(lanes, axis=1, keepdims=True)
    diagonal = lax.broadcasted_iota(jnp.int32, (QB, 128), 0) == lax.broadcasted_iota(
        jnp.int32, (QB, 128), 1
    )
    row = jnp.sum(jnp.where(diagonal, sums, 0.0), axis=0, keepdims=True)
    prow[...] = jnp.broadcast_to(row, (8, 128))
    for d in range(1, 8):
        remote(
            prow,
            zbuf.at[d - 1],
            z_s.at[d - 1],
            z_r.at[d - 1],
            (lax.rem(f + 16 * d, NF), r),
        ).start()

    for d in range(1, NR):
        part = full.at[pl.ds(behind(d) * QB, QB)]
        remote(part, part, ag_s.at[d - 1], ag_r.at[d - 1], (f, ahead(d))).wait_recv()

    def send_chunk(t, carry):
        j = lax.rem(my_j + t, HALF)
        owner = 2 * j + par
        column = jnp.maximum(tab[2 * owner + slot], 0)

        @pl.when(owner != f)
        def _():
            out[j] = full[column]
            remote(out.at[j], arrived.at[f], a_s, a_r, (owner, r)).start()

        @pl.when(owner == f)
        def _():
            arrived[f] = full[column]

        return carry

    lax.fori_loop(0, HALF, send_chunk, 0)

    for d in range(1, 8):
        remote(
            prow, zbuf.at[d - 1], z_s.at[d - 1], z_r.at[d - 1], (lax.rem(f + 16 * d, NF), r)
        ).wait()
    acc = prow[...]
    for d in range(1, 8):
        acc = acc + zbuf[d - 1]
    yrow[...] = acc
    low = lax.rem(f, 16)
    for d in range(1, 8):
        remote(
            yrow,
            ybuf.at[d - 1],
            y_s.at[d - 1],
            y_r.at[d - 1],
            (f - low + lax.rem(low + 2 * d, 16), r),
        ).start()

    weight = jnp.where(tab[2 * f + slot] >= 0, 1.0 - FACTOR_DECAY, 0.0)

    @pl.when(primary)
    def _():
        remote(
            arrived.at[pl.ds(0, NF - 1)],
            arrived.at[pl.ds(0, NF - 1)],
            a_s,
            a_r,
            (f, partner),
        ).wait_recv()
        row_id = lax.broadcasted_iota(jnp.int32, (256, 256), 0)
        col_id = lax.broadcasted_iota(jnp.int32, (256, 256), 1)
        gather_id = ((row_id >> 2) & 15) * 16 + (row_id >> 6) * 4 + (row_id & 3)
        perm = jnp.where(col_id == gather_id, 1.0, 0.0).astype(BF16)
        for g in range(8):
            moved = dot32(perm, arrived[pl.ds(16 * g, 16)].reshape(256, 128)).astype(BF16)
            for q in range(4):
                block[pl.ds(64 * g, 64), pl.ds(128 * q, 128)] = moved[64 * q : 64 * q + 64]
        remote(block, block_x, gx_s, gx_r, (f, partner)).start()
        remote(fac_b, fac_x, fx_s, fx_r, (f, partner)).wait_recv()
        grad = block[...]
        own = fac[...]
        theirs = fac_x[...].astype(F32)
        is_left = par == 0
        left = FACTOR_DECAY * jnp.where(is_left, own, theirs) + weight * outer_left(grad)
        right = FACTOR_DECAY * jnp.where(is_left, theirs, own) + weight * outer_right(grad)
        newfac[...] = jnp.where(is_left, left, right)
        pltpu.make_async_copy(newfac, newfac_out, osem.at[1]).start()
        left_root, right_root = roots_of(
            [plus_diag(left, MATRIX_EPS), plus_diag(right, MATRIX_EPS)]
        )
        halfway = dot32(left_root, grad).astype(BF16)
        precond = dot32(halfway, right_root)
        prec_sq = jnp.sum(
            jnp.sum(precond * precond, axis=0, keepdims=True), axis=1, keepdims=True
        )
        unit = (precond * (1.0 / jnp.sqrt(prec_sq + NORM_EPS))).astype(BF16)
        scatter_id = ((row_id >> 2) & 3) * 64 + (row_id >> 4) * 4 + (row_id & 3)
        perm_back = jnp.where(col_id == scatter_id, 1.0, 0.0).astype(BF16)
        for g in range(8):
            piece = jnp.concatenate(
                [unit[64 * g : 64 * g + 64, 128 * q : 128 * q + 128] for q in range(4)], axis=0
            )
            ret[pl.ds(16 * g, 16)] = dot32(perm_back, piece).astype(BF16).reshape(16, 16, 128)

        def send_back(t, carry):
            target = lax.rem(f + t, NF)
            remote(ret.at[target], retbuf.at[my_j], b_s, b_r, (target, r)).start()
            return carry

        lax.fori_loop(1, NF, send_back, 0)
        retbuf[my_j] = ret[f]

    @pl.when(other)
    def _():
        remote(block, block_x, gx_s, gx_r, (f, partner)).wait_recv()
        grad = block_x[...]

        @pl.when(par == 0)
        def _():
            newfac[...] = FACTOR_DECAY * fac[...] + weight * outer_left(grad)

        @pl.when(par == 1)
        def _():
            newfac[...] = FACTOR_DECAY * fac[...] + weight * outer_right(grad)

        pltpu.make_async_copy(newfac, newfac_out, osem.at[1]).start()

    for d in range(1, 8):
        remote(
            yrow,
            ybuf.at[d - 1],
            y_s.at[d - 1],
            y_r.at[d - 1],
            (f - low + lax.rem(low + 2 * d, 16), r),
        ).wait()
    acc = yrow[...]
    for d in range(1, 8):
        acc = acc + ybuf[d - 1]
    crow[...] = acc
    core_copy = remote(crow, cbuf, c_s, c_r, (f + 1 - 2 * f_par, r))
    core_copy.start()

    @pl.when(primary)
    def _():
        part = retbuf.at[pl.ds(0, HALF - 1)]
        remote(part, part, b_s, b_r, (f, partner)).wait_recv()

    @pl.when(other)
    def _():
        remote(retbuf, retbuf, b_s, b_r, (f, partner)).wait_recv()

    for d in range(1, NR):
        base = ahead(d) * QB

        def pack(p, carry, d=d, base=base):
            xs[d - 1, p] = retbuf[tab[2 * NF + base + p] >> 2]
            return carry

        lax.fori_loop(0, QB, pack, 0)
        remote(xs.at[d - 1], xr.at[r], x_s.at[d - 1], x_r.at[d - 1], (f, ahead(d))).start()

    def pack_own(p, carry):
        xr[r, p] = retbuf[tab[2 * NF + r * QB + p] >> 2]
        return carry

    lax.fori_loop(0, QB, pack_own, 0)

    core_copy.wait()
    total_row = (crow[...] + cbuf[...])[0:1]
    scale = jnp.sqrt(
        jnp.sum(jnp.where(diagonal, total_row, 0.0), axis=1, keepdims=True)
    )
    load_mom.wait()
    decayed = MOMENTUM_DECAY * mom[...]
    newmom[...] = decayed
    for d in range(1, NR):
        part = xr.at[behind(d)]
        remote(xs.at[d - 1], part, x_s.at[d - 1], x_r.at[d - 1], (f, ahead(d))).wait_recv()
    for p in range(QB):
        s = tab[2 * NF + r * QB + p]
        holder = 2 * (s & 1) + ((s >> 1) & 1)
        newmom[p] = newmom[p] + xr[holder, p].astype(F32) * scale[p : p + 1]
    store_mom = pltpu.make_async_copy(newmom, newmom_out, osem.at[2])
    store_mom.start()

    for copy in rs_copies:
        copy.wait_send()
    for d in range(1, NR):
        part = full.at[pl.ds(r * QB, QB)]
        remote(part, part, ag_s.at[d - 1], ag_r.at[d - 1], (f, ahead(d))).wait_send()
        remote(xs.at[d - 1], xr.at[r], x_s.at[d - 1], x_r.at[d - 1], (f, ahead(d))).wait_send()

    @pl.when(primary)
    def _():
        part = out.at[pl.ds(0, HALF - 1)]
        remote(part, part, a_s, a_r, (f, partner)).wait_send()
        part_b = ret.at[pl.ds(0, NF - 1)]
        remote(part_b, part_b, b_s, b_r, (f, partner)).wait_send()
        remote(block, block_x, gx_s, gx_r, (f, partner)).wait_send()

    @pl.when(other)
    def _():
        remote(out, out, a_s, a_r, (f, partner)).wait_send()
        remote(fac_b, fac_x, fx_s, fx_r, (f, partner)).wait_send()

    store_sec.wait()
    pltpu.make_async_copy(newfac, newfac_out, osem.at[1]).wait()
    store_mom.wait()


def tables(block_owner, block_offset):
    count = block_owner.shape[0]
    positions = jnp.arange(count, dtype=jnp.int32)
    same = block_owner[:, None] == block_owner[None, :]
    earlier = positions[None, :] < positions[:, None]
    rank = jnp.sum((same & earlier).astype(jnp.int32), axis=1)
    target = block_owner * 2 + rank
    slots = jnp.arange(2 * NF, dtype=jnp.int32)
    slot_column = (
        jnp.sum(jnp.where(target[None, :] == slots[:, None], block_offset[None, :] + 1, 0), axis=1)
        - 1
    )
    at_column = block_offset[None, :] == positions[:, None]
    column_slot = jnp.sum(jnp.where(at_column, target[None, :], 0), axis=1)
    return jnp.concatenate([slot_column, column_slot])


def chunked(array):
    columns = array.shape[1]
    tiles = array.reshape(4, columns // 128, 128).transpose(1, 0, 2)
    return tiles.reshape(columns // 512, 16, 128)


def unchunked(array):
    count = array.shape[0]
    return array.reshape(count * 4, 4, 128).transpose(1, 0, 2).reshape(4, count * 512)


def shards(replica_grads, momentum, second_moment, factor_stats, block_owner, block_offset):
    tab = tables(block_owner, block_offset)
    any_space = pl.BlockSpec(memory_space=pl.ANY)
    dma = pltpu.SemaphoreType.DMA
    outs = pl.pallas_call(
        kernel,
        out_shape=(
            jax.ShapeDtypeStruct((QB, 16, 128), F32),
            jax.ShapeDtypeStruct((QB, 16, 128), F32),
            jax.ShapeDtypeStruct((BS, BS), F32),
        ),
        in_specs=[pl.BlockSpec(memory_space=pltpu.SMEM)] + [any_space] * 4,
        out_specs=(any_space,) * 3,
        scratch_shapes=[
            pltpu.VMEM((QB, 16, 128), F32),
            pltpu.VMEM((QB, 16, 128), F32),
            pltpu.VMEM((BS, BS), F32),
            pltpu.VMEM((QB, 16, 128), F32),
            pltpu.VMEM((QB, 16, 128), F32),
            pltpu.VMEM((BS, BS), F32),
            pltpu.VMEM((QB, 16, 128), BF16),
            pltpu.VMEM((NR - 1, QB, 16, 128), BF16),
            pltpu.VMEM((NBLK, 16, 128), BF16),
            pltpu.VMEM((HALF, 16, 128), BF16),
            pltpu.VMEM((NF, 16, 128), BF16),
            pltpu.VMEM((BS, BS), BF16),
            pltpu.VMEM((BS, BS), BF16),
            pltpu.VMEM((BS, BS), BF16),
            pltpu.VMEM((BS, BS), BF16),
            pltpu.VMEM((NF, 16, 128), BF16),
            pltpu.VMEM((HALF, 16, 128), BF16),
            pltpu.VMEM((NR - 1, QB, 16, 128), BF16),
            pltpu.VMEM((NR, QB, 16, 128), BF16),
            pltpu.VMEM((8, 128), F32),
            pltpu.VMEM((7, 8, 128), F32),
            pltpu.VMEM((8, 128), F32),
            pltpu.VMEM((7, 8, 128), F32),
            pltpu.VMEM((8, 128), F32),
            pltpu.VMEM((8, 128), F32),
            dma((4,)),
            dma((3,)),
            dma((3,)),
            dma((3,)),
            dma((3,)),
            dma((3,)),
            dma,
            dma,
            dma,
            dma,
            dma,
            dma,
            dma,
            dma,
            dma((3,)),
            dma((3,)),
            dma((7,)),
            dma((7,)),
            dma((7,)),
            dma((7,)),
            dma,
            dma,
        ],
        compiler_params=pltpu.CompilerParams(
            collective_id=0, has_side_effects=True, vmem_limit_bytes=48 * 1024 * 1024
        ),
    )(
        tab,
        chunked(replica_grads[0]),
        chunked(momentum),
        chunked(second_moment),
        factor_stats[0, 0],
    )
    new_momentum, new_second, new_factors = outs
    return (unchunked(new_momentum), unchunked(new_second), new_factors[None, None])


def solution(mesh):
    placed = (
        P("rep", "fsdp", None),
        P("fsdp", "rep"),
        P("fsdp", "rep"),
        P("fsdp", "rep", None, None),
        P(),
        P(),
    )
    return jax.shard_map(
        shards,
        mesh=mesh,
        in_specs=placed,
        out_specs=(P("fsdp", "rep"), P("fsdp", "rep"), P("fsdp", "rep", None, None)),
        check_vma=False,
    )
```

```python
import jax
import jax.numpy as jnp
from jax import lax
from jax.experimental import pallas as pl
from jax.experimental.pallas import tpu as pltpu
from jax.sharding import PartitionSpec as P

FACTOR_DECAY = 0.95
MATRIX_EPS = 1e-06
ADAM_DECAY = 0.99
ADAM_EPS = 1e-08
NORM_EPS = 1e-06
MOMENTUM_DECAY = 0.9

NF = 128
NR = 4
BS = 512
NBLK = 128
QB = NBLK // NR
HALF = NF // 2
PARTS = 2
PB = QB // PARTS
NZ = 8
MESH = pl.DeviceIdType.MESH
F32 = jnp.float32
BF16 = jnp.bfloat16


def dot32(left, right):
    return jnp.dot(left, right, preferred_element_type=F32)


def outer_left(mat):
    return lax.dot_general(mat, mat, (((1,), (1,)), ((), ())), preferred_element_type=F32)


def outer_right(mat):
    return lax.dot_general(mat, mat, (((0,), (0,)), ((), ())), preferred_element_type=F32)


def eye_mask():
    return lax.broadcasted_iota(jnp.int32, (BS, BS), 0) == lax.broadcasted_iota(
        jnp.int32, (BS, BS), 1
    )


def plus_diag(mat, value):
    return mat + jnp.where(eye_mask(), value, 0.0)


def roots_of(mats):
    norms = [jnp.sum(jnp.sum(m * m, axis=0, keepdims=True), axis=1, keepdims=True) for m in mats]
    scales = [2.5 / jnp.sqrt(n) for n in norms]
    coupled0 = [z * m for z, m in zip(scales, mats)]

    def next_coupled(coupled, rounded):
        square = [dot32(m, m) for m in rounded]
        inner = [s * 0.0625 - 0.625 * m for s, m in zip(square, coupled)]
        inner_b = [e.astype(BF16) for e in inner]
        fourth = [dot32(e, e) for e in inner_b]
        rest = [(q + 3.125 * e).astype(BF16) for q, e in zip(fourth, inner)]
        return [
            dot32(w, m) + (625.0 / 256.0) * c for w, m, c in zip(rest, rounded, coupled)
        ]

    rounded0 = [m.astype(BF16) for m in coupled0]
    coupled1 = next_coupled(coupled0, rounded0)
    rounded1 = [m.astype(BF16) for m in coupled1]
    pair = [
        (dot32(a, b) - 5.0 * (c + d)) * 0.0625
        for a, b, c, d in zip(rounded0, rounded1, coupled0, coupled1)
    ]
    coupled2 = next_coupled(coupled1, rounded1)
    out = []
    for u, m, z in zip(pair, coupled2, scales):
        last = 5.0 * u - (25.0 / 16.0) * m - dot32(u.astype(BF16), m.astype(BF16))
        root = plus_diag(last * 0.25, 125.0 / 64.0) * jnp.sqrt(jnp.sqrt(z))
        out.append(root.astype(BF16))
    return out


def tables(owner, offset):
    above = lax.broadcasted_iota(jnp.int32, (NBLK, NBLK), 0)
    across = lax.broadcasted_iota(jnp.int32, (NBLK, NBLK), 1)

    def down(row):
        return jnp.broadcast_to(row, (NBLK, NBLK)).T

    same = (down(owner) == owner) & (above < across)
    target = 2 * owner + jnp.sum(jnp.where(same, 1, 0), axis=0, keepdims=True)
    target_down, offset_down = down(target), down(offset)
    rows = [
        jnp.sum(jnp.where(target_down == across + NBLK * h, offset_down + 1, 0), axis=0, keepdims=True)
        - 1
        for h in range(2)
    ]
    slot_of = jnp.sum(jnp.where(offset_down == across, target_down, 0), axis=0, keepdims=True)
    rows.append(jnp.minimum(slot_of, 2 * NF - 1))
    return rows


def kernel(
    owner_in,
    offset_in,
    grads,
    mom_in,
    sec_in,
    fac_in,
    newmom_out,
    newsec_out,
    newfac_out,
    mom,
    sec,
    fac,
    newmom,
    newsec,
    newfac,
    gv,
    gq,
    rs,
    full,
    out,
    comb,
    arrived,
    block,
    block_x,
    fac_b,
    fac_x,
    unit_s,
    ret,
    retpair,
    xs,
    xr,
    prow,
    zrow,
    zbuf,
    yrow,
    ybuf,
    trow,
    cbuf,
    tabv,
    tab,
    tsem,
    lsem,
    osem,
    rs_s,
    rs_r,
    ag_s,
    ag_r,
    fx_s,
    fx_r,
    gx_s,
    gx_r,
    a_s,
    a_r,
    m_s,
    m_r,
    l_s,
    l_r,
    b_s,
    b_r,
    t_s,
    t_r,
    x_s,
    x_r,
    z_s,
    z_r,
    y_s,
    y_r,
    c_s,
    c_r,
):
    f = lax.axis_index("fsdp")
    r = lax.axis_index("rep")
    par = lax.rem(r, 2)
    slot = lax.div(r, 2)
    partner = r + 1 - 2 * par
    f_par = lax.rem(f, 2)
    my_j = lax.div(f, 2)
    my_z = lax.div(f, 2 * NZ)
    my_y = lax.rem(lax.div(f, 2), NZ)
    mate = f + 1 - 2 * f_par
    primary = f_par == par
    other = f_par != par

    def remote(src, dst, send, recv, device):
        return pltpu.make_async_remote_copy(
            src_ref=src,
            dst_ref=dst,
            send_sem=send,
            recv_sem=recv,
            device_id=device,
            device_id_type=MESH,
        )

    def on_z(d):
        return lax.rem(my_z + d, NZ)

    def on_y(d):
        return lax.rem(my_y + d, NZ)

    def along_z(d):
        return (2 * NZ * on_z(d) + 2 * my_y + f_par, r)

    def along_y(d):
        return (2 * NZ * my_z + 2 * on_y(d) + f_par, r)

    def ahead(d):
        return lax.rem(r + d, NR)

    def behind(d):
        return lax.rem(r + NR - d, NR)

    load_g = pltpu.make_async_copy(grads, gv, lsem.at[0])
    load_sec = pltpu.make_async_copy(sec_in, sec, lsem.at[1])
    load_fac = pltpu.make_async_copy(fac_in, fac, lsem.at[2])
    load_mom = pltpu.make_async_copy(mom_in, mom, lsem.at[3])
    load_g.start()
    load_sec.start()
    load_fac.start()
    load_mom.start()

    barrier = pltpu.get_barrier_semaphore()

    def greet(device):
        pl.semaphore_signal(barrier, inc=1, device_id=device, device_id_type=MESH)

    for d in range(1, NR):
        greet((f, ahead(d)))
    greet((mate, r))

    @pl.when(primary)
    def _():
        def greet_owner(t, carry):
            greet((2 * lax.rem(my_j + t, HALF) + par, r))
            return carry

        lax.fori_loop(1, HALF, greet_owner, 0, unroll=7)

    pl.semaphore_wait(barrier, jnp.where(primary, NR + HALF - 1, NR))

    load_g.wait()
    rs_copies = []
    for h in range(PARTS):
        row = []
        for d in range(1, NR):
            copy = remote(
                gv.at[pl.ds(ahead(d) * QB + h * PB, PB)],
                rs.at[d - 1, pl.ds(h * PB, PB)],
                rs_s.at[h, d - 1],
                rs_r.at[h, d - 1],
                (f, ahead(d)),
            )
            copy.start()
            row.append(copy)
        rs_copies.append(row)
    for i, row in enumerate(tables(owner_in[...], offset_in[...])):
        tabv[i : i + 1] = row
    for i in range(3, 8):
        tabv[i : i + 1] = jnp.zeros((1, 128), jnp.int32)
    table_copy = pltpu.make_async_copy(tabv, tab, tsem)
    table_copy.start()
    load_fac.wait()

    @pl.when(other)
    def _():
        fac_b[...] = fac[...].astype(BF16)

    def gather_copy(h, d, frm=None):
        base = (r if frm is None else frm) * QB + h * PB
        return remote(
            gq.at[pl.ds(h * PB, PB)],
            full.at[pl.ds(base, PB)],
            ag_s.at[h, d - 1],
            ag_r.at[h, d - 1],
            (f, ahead(d)),
        )

    table_copy.wait()
    for h in range(PARTS):
        here = pl.ds(h * PB, PB)
        for copy in rs_copies[h]:
            copy.wait_recv()
        total = gv[pl.ds(r * QB + h * PB, PB)].astype(F32)
        for d in range(1, NR):
            total = total + rs[d - 1, here].astype(F32)
        gq[here] = total.astype(BF16)
        for d in range(1, NR):
            gather_copy(h, d).start()
    full[pl.ds(r * QB, QB)] = gq[...]

    load_sec.wait()
    wide = gq[...].astype(F32)
    second = ADAM_DECAY * sec[...] + (1.0 - ADAM_DECAY) * wide * wide
    newsec[...] = second
    store_sec = pltpu.make_async_copy(newsec, newsec_out, osem.at[0])
    store_sec.start()
    direction = wide / (jnp.sqrt(second) + ADAM_EPS)
    lanes = jnp.sum(direction * direction, axis=1)
    sums = jnp.sum(lanes, axis=1, keepdims=True)
    diagonal = lax.broadcasted_iota(jnp.int32, (QB, 128), 0) == lax.broadcasted_iota(
        jnp.int32, (QB, 128), 1
    )
    row = jnp.sum(jnp.where(diagonal, sums, 0.0), axis=0, keepdims=True)
    prow[...] = jnp.broadcast_to(row, (8, 128))
    core_copy = remote(prow, cbuf, c_s, c_r, (mate, r))
    core_copy.start()

    for h in range(PARTS):
        for d in range(1, NR):
            gather_copy(h, d, behind(d)).wait_recv()

    @pl.when(other)
    def _():
        remote(fac_b, fac_x, fx_s, fx_r, (f, partner)).start()

    def chunk_for(j):
        owner = 2 * j + par
        column = tab[lax.div(owner, HALF), lax.rem(2 * owner + slot, NBLK)]
        return full[jnp.clip(column, 0, NBLK - 1)]

    far_first = (4, 5, 3, 6, 2, 7, 1, 0)

    def hand_over(d):
        rows = pl.ds(NZ * on_z(d), NZ)
        return remote(out.at[rows], comb.at[rows, f_par], l_s.at[d], l_r.at[d], (mate, r))

    def take_over(d):
        rows = pl.ds(NZ * on_z(d), NZ)
        part = comb.at[rows, 1 - f_par]
        return remote(out.at[rows], part, l_s.at[d], l_r.at[d], (mate, r))

    @pl.when(other)
    def _():
        for d in far_first:

            def build(y, carry, z=on_z(d)):
                out[NZ * z + y] = chunk_for(NZ * z + y)
                return carry

            lax.fori_loop(0, NZ, build, 0, unroll=True)
            hand_over(d).start()

    @pl.when(primary)
    def _():
        for d in far_first:

            def build(y, carry, z=on_z(d)):
                comb[NZ * z + y, f_par] = chunk_for(NZ * z + y)
                return carry

            lax.fori_loop(0, NZ, build, 0, unroll=True)
        for d in far_first:
            take_over(d).wait_recv()

            def send(e, carry, d=d):
                j = NZ * on_z(d) + on_y(e)
                remote(comb.at[j], arrived.at[my_j], a_s, a_r, (2 * j + par, r)).start()
                return carry

            lax.fori_loop(0 if d else 1, NZ, send, 0, unroll=True)
        arrived[my_j] = comb[my_j]

    def z_copy(d):
        return remote(zrow, zbuf.at[d - 1], z_s.at[d - 1], z_r.at[d - 1], along_z(d))

    def y_copy(d):
        return remote(yrow, ybuf.at[d - 1], y_s.at[d - 1], y_r.at[d - 1], along_y(d))

    def total_copy():
        return remote(trow, trow, t_s, t_r, (mate, r))

    core_copy.wait()
    weight = jnp.where(
        tab[lax.div(f, HALF), lax.rem(2 * f + slot, NBLK)] >= 0, 1.0 - FACTOR_DECAY, 0.0
    )
    all_but_one = pl.ds(0, HALF - 1)

    @pl.when(primary)
    def _():
        zrow[...] = prow[...] + cbuf[...]
        for d in range(1, NZ):
            z_copy(d).start()
        part = arrived.at[all_but_one]
        remote(part, part, a_s, a_r, (f, partner)).wait_recv()

    row_id = lax.broadcasted_iota(jnp.int32, (256, 256), 0)
    col_id = lax.broadcasted_iota(jnp.int32, (256, 256), 1)

    @pl.when(primary)
    def _():
        gather_id = ((row_id >> 2) & 15) * 16 + (row_id >> 6) * 4 + (row_id & 3)
        perm = jnp.where(col_id == gather_id, 1.0, 0.0).astype(BF16)
        for g in range(8):
            moved = dot32(perm, arrived[pl.ds(8 * g, 8)].reshape(256, 128)).astype(BF16)
            for q in range(4):
                block[pl.ds(64 * g, 64), pl.ds(128 * q, 128)] = moved[64 * q : 64 * q + 64]
        remote(block, block_x, gx_s, gx_r, (f, partner)).start()
        for d in range(1, NZ):
            z_copy(d).wait()
        acc = zrow[...]
        for d in range(1, NZ):
            acc = acc + zbuf[d - 1]
        yrow[...] = acc
        for d in range(1, NZ):
            y_copy(d).start()
        remote(fac_b, fac_x, fx_s, fx_r, (f, partner)).wait_recv()
    @pl.when(primary)
    def _():
        grad = block[...]
        own = fac[...]
        theirs = fac_x[...].astype(F32)
        is_left = par == 0
        left = FACTOR_DECAY * jnp.where(is_left, own, theirs) + weight * outer_left(grad)
        right = FACTOR_DECAY * jnp.where(is_left, theirs, own) + weight * outer_right(grad)
        newfac[...] = jnp.where(is_left, left, right)
        pltpu.make_async_copy(newfac, newfac_out, osem.at[1]).start()
        left_root, right_root = roots_of(
            [plus_diag(left, MATRIX_EPS), plus_diag(right, MATRIX_EPS)]
        )
        halfway = dot32(left_root, grad).astype(BF16)
        precond = dot32(halfway, right_root)
        prec_sq = jnp.sum(
            jnp.sum(precond * precond, axis=0, keepdims=True), axis=1, keepdims=True
        )
        unit = (precond * (1.0 / jnp.sqrt(prec_sq + NORM_EPS))).astype(BF16)
        unit_s[...] = unit

    def share():
        return remote(
            retpair.at[:, 1 - f_par], retpair.at[:, 1 - f_par], m_s, m_r, (mate, r)
        )

    @pl.when(primary)
    def _():
        scatter_id = ((row_id >> 2) & 3) * 64 + (row_id >> 4) * 4 + (row_id & 3)
        perm_back = jnp.where(col_id == scatter_id, 1.0, 0.0).astype(BF16)
        for d in far_first:
            rows = unit_s[pl.ds(64 * on_z(d), 64), :]
            piece = jnp.concatenate([rows[:, 128 * q : 128 * q + 128] for q in range(4)], axis=0)
            moved = dot32(perm_back, piece).astype(BF16).reshape(NZ, 2, 16, 128)
            ret[pl.ds(NZ * on_z(d), NZ)] = moved

            def send_back(e, carry, d=d):
                j = NZ * on_z(d) + on_y(e)
                remote(ret.at[j], retpair.at[my_j], b_s, b_r, (2 * j + par, r)).start()
                return carry

            lax.fori_loop(0 if d else 1, NZ, send_back, 0, unroll=True)
        retpair[my_j] = ret[my_j]
        for d in range(1, NZ):
            y_copy(d).wait()
        acc = yrow[...]
        for d in range(1, NZ):
            acc = acc + ybuf[d - 1]
        trow[...] = acc
        total_copy().start()
        part = retpair.at[all_but_one]
        remote(part, part, b_s, b_r, (f, partner)).wait_recv()
        share().start()

    @pl.when(other)
    def _():
        remote(block, block_x, gx_s, gx_r, (f, partner)).wait_recv()
        grad = block_x[...]

        @pl.when(par == 0)
        def _():
            newfac[...] = FACTOR_DECAY * fac[...] + weight * outer_left(grad)

        @pl.when(par == 1)
        def _():
            newfac[...] = FACTOR_DECAY * fac[...] + weight * outer_right(grad)

        pltpu.make_async_copy(newfac, newfac_out, osem.at[1]).start()
        total_copy().wait_recv()
        remote(retpair.at[:, f_par], retpair.at[:, f_par], m_s, m_r, (mate, r)).wait_recv()

    def back_for(column):
        s = tab[2, column]
        return retpair[s >> 2, f_par]

    for d in range(1, NR):
        base = ahead(d) * QB

        def pack(p, carry, d=d, base=base):
            xs[d - 1, p] = back_for(base + p)
            return carry

        lax.fori_loop(0, QB, pack, 0, unroll=8)
        remote(xs.at[d - 1], xr.at[r], x_s.at[d - 1], x_r.at[d - 1], (f, ahead(d))).start()

    def pack_own(p, carry):
        xr[r, p] = back_for(r * QB + p)
        return carry

    lax.fori_loop(0, QB, pack_own, 0, unroll=8)

    total_row = trow[0:1]
    scale = jnp.sqrt(
        jnp.sum(jnp.where(diagonal, total_row, 0.0), axis=1, keepdims=True)
    )
    load_mom.wait()
    decayed = MOMENTUM_DECAY * mom[...]
    newmom[...] = decayed
    for d in range(1, NR):
        part = xr.at[behind(d)]
        remote(xs.at[d - 1], part, x_s.at[d - 1], x_r.at[d - 1], (f, ahead(d))).wait_recv()
    for p in range(QB):
        s = tab[2, r * QB + p]
        holder = 2 * (s & 1) + ((s >> 1) & 1)
        newmom[p] = newmom[p] + xr[holder, p].astype(F32) * scale[p : p + 1]
    store_mom = pltpu.make_async_copy(newmom, newmom_out, osem.at[2])
    store_mom.start()

    for h in range(PARTS):
        for d in range(1, NR):
            rs_copies[h][d - 1].wait_send()
            gather_copy(h, d).wait_send()
    for d in range(1, NR):
        remote(xs.at[d - 1], xr.at[r], x_s.at[d - 1], x_r.at[d - 1], (f, ahead(d))).wait_send()

    @pl.when(primary)
    def _():
        part = comb.at[all_but_one]
        remote(part, part, a_s, a_r, (f, partner)).wait_send()
        part_b = ret.at[all_but_one]
        remote(part_b, part_b, b_s, b_r, (f, partner)).wait_send()
        remote(block, block_x, gx_s, gx_r, (f, partner)).wait_send()
        total_copy().wait_send()
        share().wait_send()

    @pl.when(other)
    def _():
        for d in far_first:
            hand_over(d).wait_send()
        remote(fac_b, fac_x, fx_s, fx_r, (f, partner)).wait_send()

    store_sec.wait()
    pltpu.make_async_copy(newfac, newfac_out, osem.at[1]).wait()
    store_mom.wait()


def place(*refs):
    *arrays, sems = refs
    count = len(arrays) // 3
    ins, outs, held = arrays[:count], arrays[count : 2 * count], arrays[2 * count :]
    loads = [pltpu.make_async_copy(ins[i], held[i], sems.at[0, i]) for i in range(count)]
    stores = [pltpu.make_async_copy(held[i], outs[i], sems.at[1, i]) for i in range(count)]
    for load in loads:
        load.start()
    for load, store in zip(loads, stores):
        load.wait()
        store.start()
    for store in stores:
        store.wait()


def chunked(array):
    columns = array.shape[1]
    tiles = array.reshape(4, columns // 128, 128).transpose(1, 0, 2)
    return tiles.reshape(columns // 512, 16, 128)


def unchunked(array):
    count = array.shape[0]
    return array.reshape(count * 4, 4, 128).transpose(1, 0, 2).reshape(4, count * 512)


def shards(replica_grads, momentum, second_moment, factor_stats, block_owner, block_offset):
    hbm = pl.BlockSpec(memory_space=pltpu.HBM)
    any_space = pl.BlockSpec(memory_space=pl.ANY)
    dma = pltpu.SemaphoreType.DMA
    outs = pl.pallas_call(
        kernel,
        out_shape=(
            jax.ShapeDtypeStruct((QB, 16, 128), F32),
            jax.ShapeDtypeStruct((QB, 16, 128), F32),
            jax.ShapeDtypeStruct((BS, BS), F32),
        ),
        in_specs=[pl.BlockSpec(memory_space=pltpu.VMEM)] * 2 + [hbm] * 4,
        out_specs=(any_space,) * 3,
        scratch_shapes=[
            pltpu.VMEM((QB, 16, 128), F32),
            pltpu.VMEM((QB, 16, 128), F32),
            pltpu.VMEM((BS, BS), F32),
            pltpu.VMEM((QB, 16, 128), F32),
            pltpu.VMEM((QB, 16, 128), F32),
            pltpu.VMEM((BS, BS), F32),
            pltpu.VMEM((NBLK, 16, 128), BF16),
            pltpu.VMEM((QB, 16, 128), BF16),
            pltpu.VMEM((NR - 1, QB, 16, 128), BF16),
            pltpu.VMEM((NBLK, 16, 128), BF16),
            pltpu.VMEM((HALF, 16, 128), BF16),
            pltpu.VMEM((HALF, 2, 16, 128), BF16),
            pltpu.VMEM((HALF, 2, 16, 128), BF16),
            pltpu.VMEM((BS, BS), BF16),
            pltpu.VMEM((BS, BS), BF16),
            pltpu.VMEM((BS, BS), BF16),
            pltpu.VMEM((BS, BS), BF16),
            pltpu.VMEM((BS, BS), BF16),
            pltpu.VMEM((HALF, 2, 16, 128), BF16),
            pltpu.VMEM((HALF, 2, 16, 128), BF16),
            pltpu.VMEM((NR - 1, QB, 16, 128), BF16),
            pltpu.VMEM((NR, QB, 16, 128), BF16),
            pltpu.VMEM((8, 128), F32),
            pltpu.VMEM((8, 128), F32),
            pltpu.VMEM((7, 8, 128), F32),
            pltpu.VMEM((8, 128), F32),
            pltpu.VMEM((7, 8, 128), F32),
            pltpu.VMEM((8, 128), F32),
            pltpu.VMEM((8, 128), F32),
            pltpu.VMEM((8, 128), jnp.int32),
            pltpu.SMEM((8, 128), jnp.int32),
            dma,
            dma((4,)),
            dma((3,)),
            dma((PARTS, 3)),
            dma((PARTS, 3)),
            dma((PARTS, 3)),
            dma((PARTS, 3)),
            dma,
            dma,
            dma,
            dma,
            dma,
            dma,
            dma,
            dma,
            dma((NZ,)),
            dma((NZ,)),
            dma,
            dma,
            dma,
            dma,
            dma((3,)),
            dma((3,)),
            dma((7,)),
            dma((7,)),
            dma((7,)),
            dma((7,)),
            dma,
            dma,
        ],
        compiler_params=pltpu.CompilerParams(
            collective_id=0, has_side_effects=True, vmem_limit_bytes=60 * 1024 * 1024
        ),
    )(
        block_owner.reshape(1, NBLK),
        block_offset.reshape(1, NBLK),
        chunked(replica_grads[0]),
        chunked(momentum),
        chunked(second_moment),
        factor_stats[0, 0],
    )
    count = len(outs)
    new_momentum, new_second, new_factors = pl.pallas_call(
        place,
        out_shape=[jax.ShapeDtypeStruct(o.shape, o.dtype) for o in outs],
        in_specs=[any_space] * count,
        out_specs=[any_space] * count,
        scratch_shapes=[pltpu.VMEM(o.shape, o.dtype) for o in outs] + [dma((2, count))],
        compiler_params=pltpu.CompilerParams(vmem_limit_bytes=60 * 1024 * 1024),
    )(*outs)
    return (unchunked(new_momentum), unchunked(new_second), new_factors[None, None])


def solution(mesh):
    placed = (
        P("rep", "fsdp", None),
        P("fsdp", "rep"),
        P("fsdp", "rep"),
        P("fsdp", "rep", None, None),
        P(),
        P(),
    )
    return jax.shard_map(
        shards,
        mesh=mesh,
        in_specs=placed,
        out_specs=(P("fsdp", "rep"), P("fsdp", "rep"), P("fsdp", "rep", None, None)),
        check_vma=False,
    )
```

```python
import jax
import jax.numpy as jnp
from jax import lax
from jax.experimental import pallas as pl
from jax.experimental.pallas import tpu as pltpu
from jax.sharding import PartitionSpec as P

FACTOR_DECAY = 0.95
MATRIX_EPS = 1e-06
ADAM_DECAY = 0.99
ADAM_EPS = 1e-08
NORM_EPS = 1e-06
MOMENTUM_DECAY = 0.9

NF = 128
NR = 4
BS = 512
NBLK = 128
QB = NBLK // NR
HALF = NF // 2
PARTS = 2
PB = QB // PARTS
NZ = 8
MESH = pl.DeviceIdType.MESH
F32 = jnp.float32
BF16 = jnp.bfloat16


def dot32(left, right):
    return jnp.dot(left, right, preferred_element_type=F32)


def outer_left(mat):
    return lax.dot_general(mat, mat, (((1,), (1,)), ((), ())), preferred_element_type=F32)


def outer_right(mat):
    return lax.dot_general(mat, mat, (((0,), (0,)), ((), ())), preferred_element_type=F32)


def eye_mask():
    return lax.broadcasted_iota(jnp.int32, (BS, BS), 0) == lax.broadcasted_iota(
        jnp.int32, (BS, BS), 1
    )


def plus_diag(mat, value):
    return mat + jnp.where(eye_mask(), value, 0.0)


def roots_of(mats):
    norms = [jnp.sum(jnp.sum(m * m, axis=0, keepdims=True), axis=1, keepdims=True) for m in mats]
    scales = [2.5 / jnp.sqrt(n) for n in norms]
    coupled0 = [(0.25 * z) * m for z, m in zip(scales, mats)]

    def next_coupled(coupled, rounded):
        inner = [dot32(m, m) - 2.5 * c for m, c in zip(rounded, coupled)]
        inner_b = [e.astype(BF16) for e in inner]
        rest = [(dot32(b, b) + 3.125 * e).astype(BF16) for b, e in zip(inner_b, inner)]
        return [
            dot32(w, m) + (625.0 / 256.0) * c for w, m, c in zip(rest, rounded, coupled)
        ]

    rounded0 = [m.astype(BF16) for m in coupled0]
    coupled1 = next_coupled(coupled0, rounded0)
    rounded1 = [m.astype(BF16) for m in coupled1]
    pair = [
        dot32(a, b) - 1.25 * (c + d)
        for a, b, c, d in zip(rounded0, rounded1, coupled0, coupled1)
    ]
    coupled2 = next_coupled(coupled1, rounded1)
    out = []
    for u, m, z in zip(pair, coupled2, scales):
        last = 1.25 * u - 1.5625 * m - dot32(u.astype(BF16), m.astype(BF16))
        root = plus_diag(last, 125.0 / 64.0) * jnp.sqrt(jnp.sqrt(z))
        out.append(root.astype(BF16))
    return out


def tables(owner, offset):
    above = lax.broadcasted_iota(jnp.int32, (NBLK, NBLK), 0)
    across = lax.broadcasted_iota(jnp.int32, (NBLK, NBLK), 1)

    def down(row):
        return jnp.broadcast_to(row, (NBLK, NBLK)).T

    same = (down(owner) == owner) & (above < across)
    target = 2 * owner + jnp.sum(jnp.where(same, 1, 0), axis=0, keepdims=True)
    target_down, offset_down = down(target), down(offset)
    rows = [
        jnp.sum(jnp.where(target_down == across + NBLK * h, offset_down + 1, 0), axis=0, keepdims=True)
        - 1
        for h in range(2)
    ]
    slot_of = jnp.sum(jnp.where(offset_down == across, target_down, 0), axis=0, keepdims=True)
    rows.append(jnp.minimum(slot_of, 2 * NF - 1))
    return rows


def kernel(
    owner_in,
    offset_in,
    grads,
    mom_in,
    sec_in,
    fac_in,
    newmom_out,
    newsec_out,
    newfac_out,
    mom,
    sec,
    fac,
    newmom,
    newsec,
    newfac,
    gv,
    gq,
    rs,
    full,
    out,
    comb,
    arrived,
    block,
    block_x,
    fac_b,
    fac_x,
    unit_s,
    ret,
    retpair,
    xs,
    xr,
    prow,
    zrow,
    zbuf,
    yrow,
    ybuf,
    trow,
    cbuf,
    tabv,
    tab,
    tsem,
    lsem,
    osem,
    rs_s,
    rs_r,
    ag_s,
    ag_r,
    fx_s,
    fx_r,
    gx_s,
    gx_r,
    a_s,
    a_r,
    m_s,
    m_r,
    l_s,
    l_r,
    b_s,
    b_r,
    t_s,
    t_r,
    x_s,
    x_r,
    z_s,
    z_r,
    y_s,
    y_r,
    c_s,
    c_r,
):
    f = lax.axis_index("fsdp")
    r = lax.axis_index("rep")
    par = lax.rem(r, 2)
    slot = lax.div(r, 2)
    partner = r + 1 - 2 * par
    f_par = lax.rem(f, 2)
    my_j = lax.div(f, 2)
    my_z = lax.div(f, 2 * NZ)
    my_y = lax.rem(lax.div(f, 2), NZ)
    mate = f + 1 - 2 * f_par
    primary = f_par == par
    other = f_par != par

    def remote(src, dst, send, recv, device):
        return pltpu.make_async_remote_copy(
            src_ref=src,
            dst_ref=dst,
            send_sem=send,
            recv_sem=recv,
            device_id=device,
            device_id_type=MESH,
        )

    def on_z(d):
        return lax.rem(my_z + d, NZ)

    def on_y(d):
        return lax.rem(my_y + d, NZ)

    def along_z(d):
        return (2 * NZ * on_z(d) + 2 * my_y + f_par, r)

    def along_y(d):
        return (2 * NZ * my_z + 2 * on_y(d) + f_par, r)

    def ahead(d):
        return lax.rem(r + d, NR)

    def behind(d):
        return lax.rem(r + NR - d, NR)

    load_g = pltpu.make_async_copy(grads, gv, lsem.at[0])
    load_sec = pltpu.make_async_copy(sec_in, sec, lsem.at[1])
    load_fac = pltpu.make_async_copy(fac_in, fac, lsem.at[2])
    load_mom = pltpu.make_async_copy(mom_in, mom, lsem.at[3])
    load_g.start()
    load_sec.start()
    load_fac.start()
    load_mom.start()

    barrier = pltpu.get_barrier_semaphore()

    def greet(device):
        pl.semaphore_signal(barrier, inc=1, device_id=device, device_id_type=MESH)

    for d in range(1, NR):
        greet((f, ahead(d)))
    greet((mate, r))

    @pl.when(primary)
    def _():
        def greet_owner(t, carry):
            greet((2 * lax.rem(my_j + t, HALF) + par, r))
            return carry

        lax.fori_loop(1, HALF, greet_owner, 0, unroll=7)

    pl.semaphore_wait(barrier, jnp.where(primary, NR + HALF - 1, NR))

    load_g.wait()
    rs_copies = []
    for h in range(PARTS):
        row = []
        for d in (2, 1, 3):
            copy = remote(
                gv.at[pl.ds(ahead(d) * QB + h * PB, PB)],
                rs.at[d - 1, pl.ds(h * PB, PB)],
                rs_s.at[h, d - 1],
                rs_r.at[h, d - 1],
                (f, ahead(d)),
            )
            copy.start()
            row.append(copy)
        rs_copies.append(row)
    for i, row in enumerate(tables(owner_in[...], offset_in[...])):
        tabv[i : i + 1] = row
    for i in range(3, 8):
        tabv[i : i + 1] = jnp.zeros((1, 128), jnp.int32)
    table_copy = pltpu.make_async_copy(tabv, tab, tsem)
    table_copy.start()
    load_fac.wait()

    @pl.when(other)
    def _():
        fac_b[...] = fac[...].astype(BF16)

    def gather_copy(h, d, frm=None):
        base = (r if frm is None else frm) * QB + h * PB
        return remote(
            gq.at[pl.ds(h * PB, PB)],
            full.at[pl.ds(base, PB)],
            ag_s.at[h, d - 1],
            ag_r.at[h, d - 1],
            (f, ahead(d)),
        )

    table_copy.wait()
    for h in range(PARTS):
        here = pl.ds(h * PB, PB)
        for copy in rs_copies[h]:
            copy.wait_recv()
        total = gv[pl.ds(r * QB + h * PB, PB)].astype(F32)
        for d in range(1, NR):
            total = total + rs[d - 1, here].astype(F32)
        gq[here] = total.astype(BF16)
        for d in (2, 1, 3):
            gather_copy(h, d).start()
    full[pl.ds(r * QB, QB)] = gq[...]

    load_sec.wait()
    wide = gq[...].astype(F32)
    second = ADAM_DECAY * sec[...] + (1.0 - ADAM_DECAY) * wide * wide
    newsec[...] = second
    store_sec = pltpu.make_async_copy(newsec, newsec_out, osem.at[0])
    store_sec.start()
    direction = wide / (jnp.sqrt(second) + ADAM_EPS)
    lanes = jnp.sum(direction * direction, axis=1)
    sums = jnp.sum(lanes, axis=1, keepdims=True)
    diagonal = lax.broadcasted_iota(jnp.int32, (QB, 128), 0) == lax.broadcasted_iota(
        jnp.int32, (QB, 128), 1
    )
    row = jnp.sum(jnp.where(diagonal, sums, 0.0), axis=0, keepdims=True)
    prow[...] = jnp.broadcast_to(row, (8, 128))
    core_copy = remote(prow, cbuf, c_s, c_r, (mate, r))
    core_copy.start()

    for h in range(PARTS):
        for d in range(1, NR):
            gather_copy(h, d, behind(d)).wait_recv()

    @pl.when(other)
    def _():
        remote(fac_b, fac_x, fx_s, fx_r, (f, partner)).start()

    def chunk_for(j):
        owner = 2 * j + par
        column = tab[lax.div(owner, HALF), lax.rem(2 * owner + slot, NBLK)]
        return full[jnp.clip(column, 0, NBLK - 1)]

    far_first = (4, 5, 3, 6, 2, 7, 1, 0)

    def hand_over(d):
        rows = pl.ds(NZ * on_z(d), NZ)
        return remote(out.at[rows], comb.at[f_par, rows], l_s.at[d], l_r.at[d], (mate, r))

    def take_over(d):
        rows = pl.ds(NZ * on_z(d), NZ)
        part = comb.at[1 - f_par, rows]
        return remote(out.at[rows], part, l_s.at[d], l_r.at[d], (mate, r))

    @pl.when(other)
    def _():
        for d in far_first:

            def build(y, carry, z=on_z(d)):
                out[NZ * z + y] = chunk_for(NZ * z + y)
                return carry

            lax.fori_loop(0, NZ, build, 0, unroll=True)
            hand_over(d).start()

    @pl.when(primary)
    def _():
        for d in far_first:

            def build(y, carry, z=on_z(d)):
                comb[f_par, NZ * z + y] = chunk_for(NZ * z + y)
                return carry

            lax.fori_loop(0, NZ, build, 0, unroll=True)
        for d in far_first:
            take_over(d).wait_recv()

            def send(e, carry, d=d):
                j = NZ * on_z(d) + on_y(e)
                remote(comb.at[:, j], arrived.at[my_j], a_s, a_r, (2 * j + par, r)).start()
                return carry

            lax.fori_loop(0 if d else 1, NZ, send, 0, unroll=True)
        arrived[my_j] = comb[:, my_j]

    def z_copy(d):
        return remote(zrow, zbuf.at[d - 1], z_s.at[d - 1], z_r.at[d - 1], along_z(d))

    def y_copy(d):
        return remote(yrow, ybuf.at[d - 1], y_s.at[d - 1], y_r.at[d - 1], along_y(d))

    def total_copy():
        return remote(trow, trow, t_s, t_r, (mate, r))

    core_copy.wait()
    weight = jnp.where(
        tab[lax.div(f, HALF), lax.rem(2 * f + slot, NBLK)] >= 0, 1.0 - FACTOR_DECAY, 0.0
    )
    all_but_one = pl.ds(0, HALF - 1)

    @pl.when(primary)
    def _():
        zrow[...] = prow[...] + cbuf[...]
        for d in range(1, NZ):
            z_copy(d).start()
        part = arrived.at[all_but_one]
        remote(part, part, a_s, a_r, (f, partner)).wait_recv()

    row_id = lax.broadcasted_iota(jnp.int32, (256, 256), 0)
    col_id = lax.broadcasted_iota(jnp.int32, (256, 256), 1)

    @pl.when(primary)
    def _():
        gather_id = ((row_id >> 2) & 15) * 16 + (row_id >> 6) * 4 + (row_id & 3)
        perm = jnp.where(col_id == gather_id, 1.0, 0.0).astype(BF16)
        for g in range(8):
            moved = dot32(perm, arrived[pl.ds(8 * g, 8)].reshape(256, 128)).astype(BF16)
            for q in range(4):
                block[pl.ds(64 * g, 64), pl.ds(128 * q, 128)] = moved[64 * q : 64 * q + 64]
        remote(block, block_x, gx_s, gx_r, (f, partner)).start()
        for d in range(1, NZ):
            z_copy(d).wait()
        acc = zrow[...]
        for d in range(1, NZ):
            acc = acc + zbuf[d - 1]
        yrow[...] = acc
        for d in range(1, NZ):
            y_copy(d).start()
        remote(fac_b, fac_x, fx_s, fx_r, (f, partner)).wait_recv()
    @pl.when(primary)
    def _():
        grad = block[...]
        own = fac[...]
        theirs = fac_x[...].astype(F32)
        is_left = par == 0
        left = FACTOR_DECAY * jnp.where(is_left, own, theirs) + weight * outer_left(grad)
        right = FACTOR_DECAY * jnp.where(is_left, theirs, own) + weight * outer_right(grad)
        newfac[...] = jnp.where(is_left, left, right)
        pltpu.make_async_copy(newfac, newfac_out, osem.at[1]).start()
        left_root, right_root = roots_of(
            [plus_diag(left, MATRIX_EPS), plus_diag(right, MATRIX_EPS)]
        )
        halfway = dot32(left_root, grad).astype(BF16)
        precond = dot32(halfway, right_root)
        prec_sq = jnp.sum(
            jnp.sum(precond * precond, axis=0, keepdims=True), axis=1, keepdims=True
        )
        unit = (precond * (1.0 / jnp.sqrt(prec_sq + NORM_EPS))).astype(BF16)
        unit_s[...] = unit

    def share():
        return remote(
            retpair.at[1 - f_par], retpair.at[1 - f_par], m_s, m_r, (mate, r)
        )

    @pl.when(primary)
    def _():
        scatter_id = ((row_id >> 2) & 3) * 64 + (row_id >> 4) * 4 + (row_id & 3)
        perm_back = jnp.where(col_id == scatter_id, 1.0, 0.0).astype(BF16)
        for d in far_first:
            rows = unit_s[pl.ds(64 * on_z(d), 64), :]
            piece = jnp.concatenate([rows[:, 128 * q : 128 * q + 128] for q in range(4)], axis=0)
            moved = dot32(perm_back, piece).astype(BF16).reshape(NZ, 2, 16, 128)
            ret[pl.ds(NZ * on_z(d), NZ)] = moved

            def send_back(e, carry, d=d):
                j = NZ * on_z(d) + on_y(e)
                remote(ret.at[j], retpair.at[:, my_j], b_s, b_r, (2 * j + par, r)).start()
                return carry

            lax.fori_loop(0 if d else 1, NZ, send_back, 0, unroll=True)
        retpair[:, my_j] = ret[my_j]
        for d in range(1, NZ):
            y_copy(d).wait()
        acc = yrow[...]
        for d in range(1, NZ):
            acc = acc + ybuf[d - 1]
        trow[...] = acc
        total_copy().start()
        part = ret.at[all_but_one]
        remote(part, part, b_s, b_r, (f, partner)).wait_recv()
        share().start()

    @pl.when(other)
    def _():
        remote(block, block_x, gx_s, gx_r, (f, partner)).wait_recv()
        grad = block_x[...]

        @pl.when(par == 0)
        def _():
            newfac[...] = FACTOR_DECAY * fac[...] + weight * outer_left(grad)

        @pl.when(par == 1)
        def _():
            newfac[...] = FACTOR_DECAY * fac[...] + weight * outer_right(grad)

        pltpu.make_async_copy(newfac, newfac_out, osem.at[1]).start()
        total_copy().wait_recv()
        remote(retpair.at[f_par], retpair.at[f_par], m_s, m_r, (mate, r)).wait_recv()

    def back_for(column):
        s = tab[2, column]
        return retpair[f_par, s >> 2]

    for d in (2, 1, 3):
        base = ahead(d) * QB

        def pack(p, carry, d=d, base=base):
            xs[d - 1, p] = back_for(base + p)
            return carry

        lax.fori_loop(0, QB, pack, 0, unroll=8)
        remote(xs.at[d - 1], xr.at[r], x_s.at[d - 1], x_r.at[d - 1], (f, ahead(d))).start()

    def pack_own(p, carry):
        xr[r, p] = back_for(r * QB + p)
        return carry

    lax.fori_loop(0, QB, pack_own, 0, unroll=8)

    total_row = trow[0:1]
    scale = jnp.sqrt(
        jnp.sum(jnp.where(diagonal, total_row, 0.0), axis=1, keepdims=True)
    )
    load_mom.wait()
    decayed = MOMENTUM_DECAY * mom[...]
    newmom[...] = decayed
    for d in range(1, NR):
        part = xr.at[behind(d)]
        remote(xs.at[d - 1], part, x_s.at[d - 1], x_r.at[d - 1], (f, ahead(d))).wait_recv()
    for p in range(QB):
        s = tab[2, r * QB + p]
        holder = 2 * (s & 1) + ((s >> 1) & 1)
        newmom[p] = newmom[p] + xr[holder, p].astype(F32) * scale[p : p + 1]
    store_mom = pltpu.make_async_copy(newmom, newmom_out, osem.at[2])
    store_mom.start()

    for h in range(PARTS):
        for d in range(1, NR):
            rs_copies[h][(1, 0, 2)[d - 1]].wait_send()
            gather_copy(h, d).wait_send()
    for d in range(1, NR):
        remote(xs.at[d - 1], xr.at[r], x_s.at[d - 1], x_r.at[d - 1], (f, ahead(d))).wait_send()

    @pl.when(primary)
    def _():
        part = arrived.at[all_but_one]
        remote(part, part, a_s, a_r, (f, partner)).wait_send()
        part_b = ret.at[all_but_one]
        remote(part_b, part_b, b_s, b_r, (f, partner)).wait_send()
        remote(block, block_x, gx_s, gx_r, (f, partner)).wait_send()
        total_copy().wait_send()
        share().wait_send()

    @pl.when(other)
    def _():
        for d in far_first:
            hand_over(d).wait_send()
        remote(fac_b, fac_x, fx_s, fx_r, (f, partner)).wait_send()

    store_sec.wait()
    pltpu.make_async_copy(newfac, newfac_out, osem.at[1]).wait()
    store_mom.wait()


def place(*refs):
    *arrays, sems = refs
    count = len(arrays) // 3
    ins, outs, held = arrays[:count], arrays[count : 2 * count], arrays[2 * count :]
    loads = [pltpu.make_async_copy(ins[i], held[i], sems.at[0, i]) for i in range(count)]
    stores = [pltpu.make_async_copy(held[i], outs[i], sems.at[1, i]) for i in range(count)]
    for load in loads:
        load.start()
    for load, store in zip(loads, stores):
        load.wait()
        store.start()
    for store in stores:
        store.wait()


def chunked(array):
    columns = array.shape[1]
    tiles = array.reshape(4, columns // 128, 128).transpose(1, 0, 2)
    return tiles.reshape(columns // 512, 16, 128)


def unchunked(array):
    count = array.shape[0]
    return array.reshape(count * 4, 4, 128).transpose(1, 0, 2).reshape(4, count * 512)


def shards(replica_grads, momentum, second_moment, factor_stats, block_owner, block_offset):
    hbm = pl.BlockSpec(memory_space=pltpu.HBM)
    any_space = pl.BlockSpec(memory_space=pl.ANY)
    dma = pltpu.SemaphoreType.DMA
    outs = pl.pallas_call(
        kernel,
        out_shape=(
            jax.ShapeDtypeStruct((QB, 16, 128), F32),
            jax.ShapeDtypeStruct((QB, 16, 128), F32),
            jax.ShapeDtypeStruct((BS, BS), F32),
        ),
        in_specs=[pl.BlockSpec(memory_space=pltpu.VMEM)] * 2 + [hbm] * 4,
        out_specs=(any_space,) * 3,
        scratch_shapes=[
            pltpu.VMEM((QB, 16, 128), F32),
            pltpu.VMEM((QB, 16, 128), F32),
            pltpu.VMEM((BS, BS), F32),
            pltpu.VMEM((QB, 16, 128), F32),
            pltpu.VMEM((QB, 16, 128), F32),
            pltpu.VMEM((BS, BS), F32),
            pltpu.VMEM((NBLK, 16, 128), BF16),
            pltpu.VMEM((QB, 16, 128), BF16),
            pltpu.VMEM((NR - 1, QB, 16, 128), BF16),
            pltpu.VMEM((NBLK, 16, 128), BF16),
            pltpu.VMEM((HALF, 16, 128), BF16),
            pltpu.VMEM((2, HALF, 16, 128), BF16),
            pltpu.VMEM((HALF, 2, 16, 128), BF16),
            pltpu.VMEM((BS, BS), BF16),
            pltpu.VMEM((BS, BS), BF16),
            pltpu.VMEM((BS, BS), BF16),
            pltpu.VMEM((BS, BS), BF16),
            pltpu.VMEM((BS, BS), BF16),
            pltpu.VMEM((HALF, 2, 16, 128), BF16),
            pltpu.VMEM((2, HALF, 16, 128), BF16),
            pltpu.VMEM((NR - 1, QB, 16, 128), BF16),
            pltpu.VMEM((NR, QB, 16, 128), BF16),
            pltpu.VMEM((8, 128), F32),
            pltpu.VMEM((8, 128), F32),
            pltpu.VMEM((7, 8, 128), F32),
            pltpu.VMEM((8, 128), F32),
            pltpu.VMEM((7, 8, 128), F32),
            pltpu.VMEM((8, 128), F32),
            pltpu.VMEM((8, 128), F32),
            pltpu.VMEM((8, 128), jnp.int32),
            pltpu.SMEM((8, 128), jnp.int32),
            dma,
            dma((4,)),
            dma((3,)),
            dma((PARTS, 3)),
            dma((PARTS, 3)),
            dma((PARTS, 3)),
            dma((PARTS, 3)),
            dma,
            dma,
            dma,
            dma,
            dma,
            dma,
            dma,
            dma,
            dma((NZ,)),
            dma((NZ,)),
            dma,
            dma,
            dma,
            dma,
            dma((3,)),
            dma((3,)),
            dma((7,)),
            dma((7,)),
            dma((7,)),
            dma((7,)),
            dma,
            dma,
        ],
        compiler_params=pltpu.CompilerParams(
            collective_id=0, has_side_effects=True, vmem_limit_bytes=60 * 1024 * 1024
        ),
    )(
        block_owner.reshape(1, NBLK),
        block_offset.reshape(1, NBLK),
        chunked(replica_grads[0]),
        chunked(momentum),
        chunked(second_moment),
        factor_stats[0, 0],
    )
    count = len(outs)
    new_momentum, new_second, new_factors = pl.pallas_call(
        place,
        out_shape=[jax.ShapeDtypeStruct(o.shape, o.dtype) for o in outs],
        in_specs=[any_space] * count,
        out_specs=[any_space] * count,
        scratch_shapes=[pltpu.VMEM(o.shape, o.dtype) for o in outs] + [dma((2, count))],
        compiler_params=pltpu.CompilerParams(vmem_limit_bytes=60 * 1024 * 1024),
    )(*outs)
    return (unchunked(new_momentum), unchunked(new_second), new_factors[None, None])


def solution(mesh):
    placed = (
        P("rep", "fsdp", None),
        P("fsdp", "rep"),
        P("fsdp", "rep"),
        P("fsdp", "rep", None, None),
        P(),
        P(),
    )
    return jax.shard_map(
        shards,
        mesh=mesh,
        in_specs=placed,
        out_specs=(P("fsdp", "rep"), P("fsdp", "rep"), P("fsdp", "rep", None, None)),
        check_vma=False,
    )
```

```python
import jax
import jax.numpy as jnp
from jax import lax
from jax.experimental import pallas as pl
from jax.experimental.pallas import tpu as pltpu
from jax.sharding import PartitionSpec as P

FACTOR_DECAY = 0.95
MATRIX_EPS = 1e-06
ADAM_DECAY = 0.99
ADAM_EPS = 1e-08
NORM_EPS = 1e-06
MOMENTUM_DECAY = 0.9

NF = 128
NR = 4
BS = 512
NBLK = 128
QB = NBLK // NR
HALF = NF // 2
PARTS = 2
PB = QB // PARTS
NZ = 8
MESH = pl.DeviceIdType.MESH
F32 = jnp.float32
BF16 = jnp.bfloat16


def dot32(left, right):
    return jnp.dot(left, right, preferred_element_type=F32)


def outer_left(mat):
    return lax.dot_general(mat, mat, (((1,), (1,)), ((), ())), preferred_element_type=F32)


def outer_right(mat):
    return lax.dot_general(mat, mat, (((0,), (0,)), ((), ())), preferred_element_type=F32)


def eye_mask():
    return lax.broadcasted_iota(jnp.int32, (BS, BS), 0) == lax.broadcasted_iota(
        jnp.int32, (BS, BS), 1
    )


def plus_diag(mat, value):
    return mat + jnp.where(eye_mask(), value, 0.0)


def roots_of(mats):
    norms = [jnp.sum(jnp.sum(m * m, axis=0, keepdims=True), axis=1, keepdims=True) for m in mats]
    scales = [2.5 / jnp.sqrt(n) for n in norms]
    coupled0 = [(0.25 * z) * m for z, m in zip(scales, mats)]

    def next_coupled(coupled, rounded):
        inner = [dot32(m, m) - 2.5 * c for m, c in zip(rounded, coupled)]
        inner_b = [e.astype(BF16) for e in inner]
        rest = [(dot32(b, b) + 3.125 * e).astype(BF16) for b, e in zip(inner_b, inner)]
        return [
            dot32(w, m) + (625.0 / 256.0) * c for w, m, c in zip(rest, rounded, coupled)
        ]

    rounded0 = [m.astype(BF16) for m in coupled0]
    coupled1 = next_coupled(coupled0, rounded0)
    rounded1 = [m.astype(BF16) for m in coupled1]
    pair = [
        dot32(a, b) - 1.25 * (c + d)
        for a, b, c, d in zip(rounded0, rounded1, coupled0, coupled1)
    ]
    coupled2 = next_coupled(coupled1, rounded1)
    out = []
    for u, m, z in zip(pair, coupled2, scales):
        last = 1.25 * u - 1.5625 * m - dot32(u.astype(BF16), m.astype(BF16))
        root = plus_diag(last, 125.0 / 64.0) * jnp.sqrt(jnp.sqrt(z))
        out.append(root.astype(BF16))
    return out


def tables(owner, offset):
    above = lax.broadcasted_iota(jnp.int32, (NBLK, NBLK), 0)
    across = lax.broadcasted_iota(jnp.int32, (NBLK, NBLK), 1)

    def down(row):
        return jnp.broadcast_to(row, (NBLK, NBLK)).T

    same = (down(owner) == owner) & (above < across)
    target = 2 * owner + jnp.sum(jnp.where(same, 1, 0), axis=0, keepdims=True)
    target_down, offset_down = down(target), down(offset)
    rows = [
        jnp.sum(jnp.where(target_down == across + NBLK * h, offset_down + 1, 0), axis=0, keepdims=True)
        - 1
        for h in range(2)
    ]
    slot_of = jnp.sum(jnp.where(offset_down == across, target_down, 0), axis=0, keepdims=True)
    rows.append(jnp.minimum(slot_of, 2 * NF - 1))
    return rows


def kernel(
    owner_in,
    offset_in,
    grads,
    mom_in,
    sec_in,
    fac_in,
    newmom_out,
    newsec_out,
    newfac_out,
    mom,
    sec,
    fac,
    newmom,
    newsec,
    newfac,
    gv,
    gq,
    rs,
    full,
    out,
    comb,
    arrived,
    block,
    block_x,
    fac_b,
    fac_x,
    unit_s,
    ret,
    retpair,
    xs,
    xr,
    prow,
    zrow,
    zbuf,
    yrow,
    ybuf,
    trow,
    cbuf,
    tabv,
    tab,
    tsem,
    lsem,
    osem,
    rs_s,
    rs_r,
    ag_s,
    ag_r,
    fx_s,
    fx_r,
    gx_s,
    gx_r,
    a_s,
    a_r,
    m_s,
    m_r,
    l_s,
    l_r,
    b_s,
    b_r,
    t_s,
    t_r,
    x_s,
    x_r,
    z_s,
    z_r,
    y_s,
    y_r,
    c_s,
    c_r,
):
    f = lax.axis_index("fsdp")
    r = lax.axis_index("rep")
    par = lax.rem(r, 2)
    slot = lax.div(r, 2)
    partner = r + 1 - 2 * par
    f_par = lax.rem(f, 2)
    my_j = lax.div(f, 2)
    my_z = lax.div(f, 2 * NZ)
    my_y = lax.rem(lax.div(f, 2), NZ)
    mate = f + 1 - 2 * f_par
    primary = f_par == par
    other = f_par != par

    def remote(src, dst, send, recv, device):
        return pltpu.make_async_remote_copy(
            src_ref=src,
            dst_ref=dst,
            send_sem=send,
            recv_sem=recv,
            device_id=device,
            device_id_type=MESH,
        )

    def on_z(d):
        return lax.rem(my_z + d, NZ)

    def on_y(d):
        return lax.rem(my_y + d, NZ)

    def along_z(d):
        return (2 * NZ * on_z(d) + 2 * my_y + f_par, r)

    def along_y(d):
        return (2 * NZ * my_z + 2 * on_y(d) + f_par, r)

    def ahead(d):
        return lax.rem(r + d, NR)

    def behind(d):
        return lax.rem(r + NR - d, NR)

    load_g = pltpu.make_async_copy(grads, gv, lsem.at[0])
    load_sec = pltpu.make_async_copy(sec_in, sec, lsem.at[1])
    load_fac = pltpu.make_async_copy(fac_in, fac, lsem.at[2])
    load_mom = pltpu.make_async_copy(mom_in, mom, lsem.at[3])
    load_g.start()
    load_sec.start()
    load_fac.start()
    load_mom.start()

    barrier = pltpu.get_barrier_semaphore()

    def greet(device):
        pl.semaphore_signal(barrier, inc=1, device_id=device, device_id_type=MESH)

    for d in range(1, NR):
        greet((f, ahead(d)))
    greet((mate, r))

    @pl.when(primary)
    def _():
        def greet_owner(t, carry):
            greet((2 * lax.rem(my_j + t, HALF) + par, r))
            return carry

        lax.fori_loop(1, HALF, greet_owner, 0, unroll=7)

    pl.semaphore_wait(barrier, jnp.where(primary, NR + HALF - 1, NR))

    load_g.wait()
    rs_copies = []
    for h in range(PARTS):
        row = []
        for d in (2, 1, 3):
            copy = remote(
                gv.at[pl.ds(ahead(d) * QB + h * PB, PB)],
                rs.at[d - 1, pl.ds(h * PB, PB)],
                rs_s.at[h, d - 1],
                rs_r.at[h, d - 1],
                (f, ahead(d)),
            )
            copy.start()
            row.append(copy)
        rs_copies.append(row)
    for i, row in enumerate(tables(owner_in[...], offset_in[...])):
        tabv[i : i + 1] = row
    for i in range(3, 8):
        tabv[i : i + 1] = jnp.zeros((1, 128), jnp.int32)
    table_copy = pltpu.make_async_copy(tabv, tab, tsem)
    table_copy.start()
    load_fac.wait()

    @pl.when(other)
    def _():
        fac_b[...] = fac[...].astype(BF16)

    def gather_copy(h, d, frm=None):
        base = (r if frm is None else frm) * QB + h * PB
        return remote(
            gq.at[pl.ds(h * PB, PB)],
            full.at[pl.ds(base, PB)],
            ag_s.at[h, d - 1],
            ag_r.at[h, d - 1],
            (f, ahead(d)),
        )

    table_copy.wait()
    for h in range(PARTS):
        here = pl.ds(h * PB, PB)
        for copy in rs_copies[h]:
            copy.wait_recv()
        total = gv[pl.ds(r * QB + h * PB, PB)].astype(F32)
        for d in range(1, NR):
            total = total + rs[d - 1, here].astype(F32)
        gq[here] = total.astype(BF16)
        for d in (2, 1, 3):
            gather_copy(h, d).start()
    full[pl.ds(r * QB, QB)] = gq[...]

    load_sec.wait()
    wide = gq[...].astype(F32)
    second = ADAM_DECAY * sec[...] + (1.0 - ADAM_DECAY) * wide * wide
    newsec[...] = second
    store_sec = pltpu.make_async_copy(newsec, newsec_out, osem.at[0])
    store_sec.start()
    direction = wide / (jnp.sqrt(second) + ADAM_EPS)
    lanes = jnp.sum(direction * direction, axis=1)
    sums = jnp.sum(lanes, axis=1, keepdims=True)
    diagonal = lax.broadcasted_iota(jnp.int32, (QB, 128), 0) == lax.broadcasted_iota(
        jnp.int32, (QB, 128), 1
    )
    row = jnp.sum(jnp.where(diagonal, sums, 0.0), axis=0, keepdims=True)
    prow[...] = jnp.broadcast_to(row, (8, 128))
    core_copy = remote(prow, cbuf, c_s, c_r, (mate, r))
    core_copy.start()

    for h in range(PARTS):
        for d in range(1, NR):
            gather_copy(h, d, behind(d)).wait_recv()

    def chunk_for(j):
        owner = 2 * j + par
        column = tab[lax.div(owner, HALF), lax.rem(2 * owner + slot, NBLK)]
        return full[jnp.clip(column, 0, NBLK - 1)]

    far_first = (4, 5, 3, 6, 2, 7, 1, 0)

    def hand_over(d):
        rows = pl.ds(NZ * on_z(d), NZ)
        return remote(out.at[rows], comb.at[f_par, rows], l_s.at[d], l_r.at[d], (mate, r))

    def take_over(d):
        rows = pl.ds(NZ * on_z(d), NZ)
        part = comb.at[1 - f_par, rows]
        return remote(out.at[rows], part, l_s.at[d], l_r.at[d], (mate, r))

    @pl.when(other)
    def _():
        for d in far_first:

            def build(y, carry, z=on_z(d)):
                out[NZ * z + y] = chunk_for(NZ * z + y)
                return carry

            lax.fori_loop(0, NZ, build, 0, unroll=True)
            hand_over(d).start()
        remote(fac_b, fac_x, fx_s, fx_r, (f, partner)).start()

    @pl.when(primary)
    def _():
        for d in far_first:

            def build(y, carry, z=on_z(d)):
                comb[f_par, NZ * z + y] = chunk_for(NZ * z + y)
                return carry

            lax.fori_loop(0, NZ, build, 0, unroll=True)
        for d in far_first:
            take_over(d).wait_recv()

            def send(e, carry, d=d):
                j = NZ * on_z(d) + on_y(e)
                remote(comb.at[:, j], arrived.at[my_j], a_s, a_r, (2 * j + par, r)).start()
                return carry

            lax.fori_loop(0 if d else 1, NZ, send, 0, unroll=True)
        arrived[my_j] = comb[:, my_j]

    def z_copy(d):
        return remote(zrow, zbuf.at[d - 1], z_s.at[d - 1], z_r.at[d - 1], along_z(d))

    def y_copy(d):
        return remote(yrow, ybuf.at[d - 1], y_s.at[d - 1], y_r.at[d - 1], along_y(d))

    def total_copy():
        return remote(trow, trow, t_s, t_r, (mate, r))

    core_copy.wait()
    weight = jnp.where(
        tab[lax.div(f, HALF), lax.rem(2 * f + slot, NBLK)] >= 0, 1.0 - FACTOR_DECAY, 0.0
    )
    all_but_one = pl.ds(0, HALF - 1)

    @pl.when(primary)
    def _():
        zrow[...] = prow[...] + cbuf[...]
        for d in range(1, NZ):
            z_copy(d).start()
        part = arrived.at[all_but_one]
        remote(part, part, a_s, a_r, (f, partner)).wait_recv()

    row_id = lax.broadcasted_iota(jnp.int32, (256, 256), 0)
    col_id = lax.broadcasted_iota(jnp.int32, (256, 256), 1)

    @pl.when(primary)
    def _():
        gather_id = ((row_id >> 2) & 15) * 16 + (row_id >> 6) * 4 + (row_id & 3)
        perm = jnp.where(col_id == gather_id, 1.0, 0.0).astype(BF16)
        for g in range(8):
            moved = dot32(perm, arrived[pl.ds(8 * g, 8)].reshape(256, 128)).astype(BF16)
            for q in range(4):
                block[pl.ds(64 * g, 64), pl.ds(128 * q, 128)] = moved[64 * q : 64 * q + 64]
        remote(block, block_x, gx_s, gx_r, (f, partner)).start()
        for d in range(1, NZ):
            z_copy(d).wait()
        acc = zrow[...]
        for d in range(1, NZ):
            acc = acc + zbuf[d - 1]
        yrow[...] = acc
        for d in range(1, NZ):
            y_copy(d).start()
        remote(fac_b, fac_x, fx_s, fx_r, (f, partner)).wait_recv()
    @pl.when(primary)
    def _():
        grad = block[...]
        own = fac[...]
        theirs = fac_x[...].astype(F32)
        is_left = par == 0
        left = FACTOR_DECAY * jnp.where(is_left, own, theirs) + weight * outer_left(grad)
        right = FACTOR_DECAY * jnp.where(is_left, theirs, own) + weight * outer_right(grad)
        newfac[...] = jnp.where(is_left, left, right)
        pltpu.make_async_copy(newfac, newfac_out, osem.at[1]).start()
        left_root, right_root = roots_of(
            [plus_diag(left, MATRIX_EPS), plus_diag(right, MATRIX_EPS)]
        )
        halfway = dot32(left_root, grad).astype(BF16)
        precond = dot32(halfway, right_root)
        prec_sq = jnp.sum(
            jnp.sum(precond * precond, axis=0, keepdims=True), axis=1, keepdims=True
        )
        unit = (precond * (1.0 / jnp.sqrt(prec_sq + NORM_EPS))).astype(BF16)
        unit_s[...] = unit

    def share():
        return remote(
            retpair.at[1 - f_par], retpair.at[1 - f_par], m_s, m_r, (mate, r)
        )

    @pl.when(primary)
    def _():
        scatter_id = ((row_id >> 2) & 3) * 64 + (row_id >> 4) * 4 + (row_id & 3)
        perm_back = jnp.where(col_id == scatter_id, 1.0, 0.0).astype(BF16)
        for d in far_first:
            rows = unit_s[pl.ds(64 * on_z(d), 64), :]
            piece = jnp.concatenate([rows[:, 128 * q : 128 * q + 128] for q in range(4)], axis=0)
            moved = dot32(perm_back, piece).astype(BF16).reshape(NZ, 2, 16, 128)
            ret[pl.ds(NZ * on_z(d), NZ)] = moved

            def send_back(e, carry, d=d):
                j = NZ * on_z(d) + on_y(e)
                remote(ret.at[j], retpair.at[:, my_j], b_s, b_r, (2 * j + par, r)).start()
                return carry

            lax.fori_loop(0 if d else 1, NZ, send_back, 0, unroll=True)
        retpair[:, my_j] = ret[my_j]
        for d in range(1, NZ):
            y_copy(d).wait()
        acc = yrow[...]
        for d in range(1, NZ):
            acc = acc + ybuf[d - 1]
        trow[...] = acc
        total_copy().start()
        part = ret.at[all_but_one]
        remote(part, part, b_s, b_r, (f, partner)).wait_recv()
        share().start()

    @pl.when(other)
    def _():
        remote(block, block_x, gx_s, gx_r, (f, partner)).wait_recv()
        grad = block_x[...]

        @pl.when(par == 0)
        def _():
            newfac[...] = FACTOR_DECAY * fac[...] + weight * outer_left(grad)

        @pl.when(par == 1)
        def _():
            newfac[...] = FACTOR_DECAY * fac[...] + weight * outer_right(grad)

        pltpu.make_async_copy(newfac, newfac_out, osem.at[1]).start()
        total_copy().wait_recv()
        remote(retpair.at[f_par], retpair.at[f_par], m_s, m_r, (mate, r)).wait_recv()

    def back_for(column):
        s = tab[2, column]
        return retpair[f_par, s >> 2]

    for d in (2, 1, 3):
        base = ahead(d) * QB

        def pack(p, carry, d=d, base=base):
            xs[d - 1, p] = back_for(base + p)
            return carry

        lax.fori_loop(0, QB, pack, 0, unroll=8)
        remote(xs.at[d - 1], xr.at[r], x_s.at[d - 1], x_r.at[d - 1], (f, ahead(d))).start()

    def pack_own(p, carry):
        xr[r, p] = back_for(r * QB + p)
        return carry

    lax.fori_loop(0, QB, pack_own, 0, unroll=8)

    total_row = trow[0:1]
    scale = jnp.sqrt(
        jnp.sum(jnp.where(diagonal, total_row, 0.0), axis=1, keepdims=True)
    )
    load_mom.wait()
    decayed = MOMENTUM_DECAY * mom[...]
    newmom[...] = decayed
    for d in range(1, NR):
        part = xr.at[behind(d)]
        remote(xs.at[d - 1], part, x_s.at[d - 1], x_r.at[d - 1], (f, ahead(d))).wait_recv()
    for p in range(QB):
        s = tab[2, r * QB + p]
        holder = 2 * (s & 1) + ((s >> 1) & 1)
        newmom[p] = newmom[p] + xr[holder, p].astype(F32) * scale[p : p + 1]
    store_mom = pltpu.make_async_copy(newmom, newmom_out, osem.at[2])
    store_mom.start()

    for h in range(PARTS):
        for d in range(1, NR):
            rs_copies[h][(1, 0, 2)[d - 1]].wait_send()
            gather_copy(h, d).wait_send()
    for d in range(1, NR):
        remote(xs.at[d - 1], xr.at[r], x_s.at[d - 1], x_r.at[d - 1], (f, ahead(d))).wait_send()

    @pl.when(primary)
    def _():
        part = arrived.at[all_but_one]
        remote(part, part, a_s, a_r, (f, partner)).wait_send()
        part_b = ret.at[all_but_one]
        remote(part_b, part_b, b_s, b_r, (f, partner)).wait_send()
        remote(block, block_x, gx_s, gx_r, (f, partner)).wait_send()
        total_copy().wait_send()
        share().wait_send()

    @pl.when(other)
    def _():
        for d in far_first:
            hand_over(d).wait_send()
        remote(fac_b, fac_x, fx_s, fx_r, (f, partner)).wait_send()

    store_sec.wait()
    pltpu.make_async_copy(newfac, newfac_out, osem.at[1]).wait()
    store_mom.wait()


def place(*refs):
    *arrays, sems = refs
    count = len(arrays) // 3
    ins, outs, held = arrays[:count], arrays[count : 2 * count], arrays[2 * count :]
    loads = [pltpu.make_async_copy(ins[i], held[i], sems.at[0, i]) for i in range(count)]
    stores = [pltpu.make_async_copy(held[i], outs[i], sems.at[1, i]) for i in range(count)]
    for load in loads:
        load.start()
    for load, store in zip(loads, stores):
        load.wait()
        store.start()
    for store in stores:
        store.wait()


def chunked(array):
    columns = array.shape[1]
    tiles = array.reshape(4, columns // 128, 128).transpose(1, 0, 2)
    return tiles.reshape(columns // 512, 16, 128)


def unchunked(array):
    count = array.shape[0]
    return array.reshape(count * 4, 4, 128).transpose(1, 0, 2).reshape(4, count * 512)


def shards(replica_grads, momentum, second_moment, factor_stats, block_owner, block_offset):
    hbm = pl.BlockSpec(memory_space=pltpu.HBM)
    any_space = pl.BlockSpec(memory_space=pl.ANY)
    dma = pltpu.SemaphoreType.DMA
    outs = pl.pallas_call(
        kernel,
        out_shape=(
            jax.ShapeDtypeStruct((QB, 16, 128), F32),
            jax.ShapeDtypeStruct((QB, 16, 128), F32),
            jax.ShapeDtypeStruct((BS, BS), F32),
        ),
        in_specs=[pl.BlockSpec(memory_space=pltpu.VMEM)] * 2 + [hbm] * 4,
        out_specs=(any_space,) * 3,
        scratch_shapes=[
            pltpu.VMEM((QB, 16, 128), F32),
            pltpu.VMEM((QB, 16, 128), F32),
            pltpu.VMEM((BS, BS), F32),
            pltpu.VMEM((QB, 16, 128), F32),
            pltpu.VMEM((QB, 16, 128), F32),
            pltpu.VMEM((BS, BS), F32),
            pltpu.VMEM((NBLK, 16, 128), BF16),
            pltpu.VMEM((QB, 16, 128), BF16),
            pltpu.VMEM((NR - 1, QB, 16, 128), BF16),
            pltpu.VMEM((NBLK, 16, 128), BF16),
            pltpu.VMEM((HALF, 16, 128), BF16),
            pltpu.VMEM((2, HALF, 16, 128), BF16),
            pltpu.VMEM((HALF, 2, 16, 128), BF16),
            pltpu.VMEM((BS, BS), BF16),
            pltpu.VMEM((BS, BS), BF16),
            pltpu.VMEM((BS, BS), BF16),
            pltpu.VMEM((BS, BS), BF16),
            pltpu.VMEM((BS, BS), BF16),
            pltpu.VMEM((HALF, 2, 16, 128), BF16),
            pltpu.VMEM((2, HALF, 16, 128), BF16),
            pltpu.VMEM((NR - 1, QB, 16, 128), BF16),
            pltpu.VMEM((NR, QB, 16, 128), BF16),
            pltpu.VMEM((8, 128), F32),
            pltpu.VMEM((8, 128), F32),
            pltpu.VMEM((7, 8, 128), F32),
            pltpu.VMEM((8, 128), F32),
            pltpu.VMEM((7, 8, 128), F32),
            pltpu.VMEM((8, 128), F32),
            pltpu.VMEM((8, 128), F32),
            pltpu.VMEM((8, 128), jnp.int32),
            pltpu.SMEM((8, 128), jnp.int32),
            dma,
            dma((4,)),
            dma((3,)),
            dma((PARTS, 3)),
            dma((PARTS, 3)),
            dma((PARTS, 3)),
            dma((PARTS, 3)),
            dma,
            dma,
            dma,
            dma,
            dma,
            dma,
            dma,
            dma,
            dma((NZ,)),
            dma((NZ,)),
            dma,
            dma,
            dma,
            dma,
            dma((3,)),
            dma((3,)),
            dma((7,)),
            dma((7,)),
            dma((7,)),
            dma((7,)),
            dma,
            dma,
        ],
        compiler_params=pltpu.CompilerParams(
            collective_id=0, has_side_effects=True, vmem_limit_bytes=60 * 1024 * 1024
        ),
    )(
        block_owner.reshape(1, NBLK),
        block_offset.reshape(1, NBLK),
        chunked(replica_grads[0]),
        chunked(momentum),
        chunked(second_moment),
        factor_stats[0, 0],
    )
    count = len(outs)
    new_momentum, new_second, new_factors = pl.pallas_call(
        place,
        out_shape=[jax.ShapeDtypeStruct(o.shape, o.dtype) for o in outs],
        in_specs=[any_space] * count,
        out_specs=[any_space] * count,
        scratch_shapes=[pltpu.VMEM(o.shape, o.dtype) for o in outs] + [dma((2, count))],
        compiler_params=pltpu.CompilerParams(vmem_limit_bytes=60 * 1024 * 1024),
    )(*outs)
    return (unchunked(new_momentum), unchunked(new_second), new_factors[None, None])


def solution(mesh):
    placed = (
        P("rep", "fsdp", None),
        P("fsdp", "rep"),
        P("fsdp", "rep"),
        P("fsdp", "rep", None, None),
        P(),
        P(),
    )
    return jax.shard_map(
        shards,
        mesh=mesh,
        in_specs=placed,
        out_specs=(P("fsdp", "rep"), P("fsdp", "rep"), P("fsdp", "rep", None, None)),
        check_vma=False,
    )
```
